32 devices in a mesh: parts: 2 (over y), rep: 4 (over x, core), tp: 4 (over z).
Axes of the slice: x: 2, y: 2, z: 4, core: 2. Of those that a mesh axis runs over, the one named last changes fastest.
Arguments:
- queries: bfloat16 [192, 8192], P(('parts', 'rep'), 'tp'), parts along dimension 0, may hold values from -16 to 16, as said below
- new_kv: bfloat16 [192, 2048], P(('parts', 'rep'), 'tp'), parts along dimension 0, may hold values from -6 to 6
- kv_cache: bfloat16 [8, 96, 16, 2048], P(('parts', 'rep'), 'tp'), parts along dimension 0, may hold values from -16 to 16, as said below
- slot_owner: int32 [8, 96], P(('parts', 'rep'), 'tp'), parts along dimension 0, may hold values from -1 to 23
- slot_fill: int32 [8, 96], P(('parts', 'rep'), 'tp'), parts along dimension 0, may hold values from 1 to 16
- mig_source: int32 [8, 8], P(('parts', 'rep'), 'tp'), parts along dimension 0, may hold values from 0 to 3, as said below
- mig_slot: int32 [8, 8], P(('parts', 'rep'), 'tp'), parts along dimension 0, may hold values from 0 to 21
- adapter_id: int32 [192], P(('parts', 'rep')), parts along dimension 0, may hold values from 0 to 63
- out_weight: bfloat16 [8192, 8192], P('tp'), may hold values from -0.75 to 0.75
- shrink_weight: bfloat16 [64, 8192, 32], P(None, 'tp'), may hold values from -0.5 to 0.5
- expand_weight: bfloat16 [64, 32, 8192], P(None, None, 'tp'), may hold values from -0.5 to 0.5
Outputs:
- mixed: bfloat16 [192, 8192], P(('parts', 'rep'), 'tp'), parts along dimension 0
The draws below stay inside these ranges and needn't reach their ends.
There are 2 independent parts, one for each index of `parts`. The reference program is written for one: setup_inputs(seed, part) draws one part's arguments, and reference() takes and returns one part's arrays. A program takes and returns all parts, laid end to end along the dimension named above; an argument that names none is the same for every part. Nothing has to cross between parts.
Inputs may be any that keep to these rules, and one draw needn't show every extreme that they name: queries stay within the range. `kv_cache`: cache entries stay within the range. `mig_source`: never the replica that receives the copy.
All inputs are finite; a program needn't handle non-finite values.
Results may differ from the reference program's by a relative error of at most 0.0053.
Values may be sent and summed in bfloat16 or wider, within the bound.
A program may use at most 128 MiB of HBM per device.

```python
import math
import jax
import jax.numpy as jnp
import numpy as np
from jax import lax

D = 8192
H = 64
KVH = 8
HS = 128
RANK = 32
ADAPTERS = 64
ROWS_REP = 24
POOL = 24
BLK = 16
MIGS = 2
ROWS = 96
N_REP = 4
N_TP = 4


def draw_queries(key, part):
    key = jax.random.fold_in(key, 5)
    noise_random_key = jax.random.fold_in(key, 0)
    result = jax.random.normal(noise_random_key, (ROWS, KVH, H // KVH, HS))
    return jnp.clip(result, -16.0, 16.0).reshape(ROWS, H * HS).astype(jnp.bfloat16)


def draw_kv_cache(key, part):
    key = jax.random.fold_in(key, 7)
    shape = (N_REP, N_TP * POOL, BLK, KVH, 2, HS)
    noise_part = jax.random.normal(key, shape)
    result = noise_part
    return jnp.clip(result, -16.0, 16.0).reshape(N_REP, N_TP * POOL, BLK, 2 * KVH * HS).astype(jnp.bfloat16)


def draw_mig_source(key, part):
    key = jax.random.fold_in(key, 9)
    replica = jnp.arange(N_REP, dtype=jnp.int32)[:, None]
    offset = jax.random.randint(key, (N_REP, N_TP * MIGS), 1, N_REP, dtype=jnp.int32)
    return ((replica + offset) % N_REP).astype(jnp.int32)


def with_ends(values, rng, low, largest):
    spot = [jax.random.randint(jax.random.fold_in(rng, axis), (), 0, length) for axis, length in enumerate(values.shape)]
    main_axis = values.shape.index(max(values.shape))
    beside = spot[:main_axis] + [(spot[main_axis] + 1) % values.shape[main_axis]] + spot[main_axis + 1:]
    return values.at[tuple(spot)].set(low).at[tuple(beside)].set(largest)


def spiked(values, own_key, source, target, shards_of, factor):
    owner, partner = [(jnp.arange(values.shape[axis_at]) // (values.shape[axis_at] // shards_of)).reshape([-1 if axis == axis_at else 1 for axis in range(values.ndim)]) for axis_at in (source, target)]
    chosen = jax.random.permutation(own_key, shards_of)[partner]
    strong = (owner == chosen) | (owner == (partner + shards_of // 2) % shards_of)
    return jnp.where(strong, factor * values, values)


def block_scale(stream_key, extent, cuts, smallest, high):
    def one(dim, blocks):
        steps = jax.random.uniform(jax.random.fold_in(jax.random.fold_in(stream_key, 6), dim), (blocks,), jnp.float32, smallest / len(cuts), high / len(cuts))
        return jnp.repeat(jnp.exp(steps), extent[dim] // blocks).reshape((-1,) + (1,) * (len(extent) - dim - 1))

    loudness = one(*cuts[0])
    for cut in cuts[1:]:
        loudness = loudness * one(*cut)
    return loudness


def rank_table(number_of, skew):
    weights = [(1 << 20) // math.isqrt(standing ** skew) + 1 for standing in range(1, number_of + 1)]
    scale = 1 + sum(weights) // (1 << 30)
    return np.cumsum(np.array([max(1, weight // scale) for weight in weights]))


def ranked(rng, shape, number_of, skew):
    table = rank_table(number_of, skew)
    lot = jax.random.randint(jax.random.fold_in(rng, 1), shape, 0, int(table[number_of - 1]))
    rank = jnp.searchsorted(jnp.asarray(table, jnp.int32), lot, side="right")
    return jax.random.permutation(jax.random.fold_in(rng, 2), number_of)[rank].astype(jnp.int32)


def centred(own_key, extent, scale, reach, pieces=(), held_as=jnp.bfloat16):
    entries = scale * jax.random.normal(own_key, extent, jnp.float32)
    if pieces:
        entries = entries * block_scale(own_key, extent, pieces, -0.22, 0.18)
    return jnp.clip(entries, -reach, reach).astype(held_as)


def gaussian_with(key, shape, scale, most, cuts, heavy, kind=jnp.bfloat16):
    values = scale * jax.random.normal(key, shape, jnp.float32)
    if cuts:
        values = values * block_scale(key, shape, cuts, -0.22, 0.18)
    return jnp.clip(spiked(values, jax.random.fold_in(key, 3), *heavy), -most, most).astype(kind)


def setup_inputs(seed: int = 0, part: int = 0) -> dict:
    arg_keys = jax.random.split(jax.random.key(seed), 12)
    own_keys = jax.random.split(jax.random.fold_in(arg_keys[11], part), 12)
    return {
        "queries": draw_queries(jax.random.fold_in(jax.random.fold_in(arg_keys[11], part), 71), part),
        "new_kv": centred(own_keys[1], (ROWS, 2 * KVH * HS), 1.0, 6.0, ((0, 4), (1, 4))),
        "kv_cache": draw_kv_cache(jax.random.fold_in(jax.random.fold_in(arg_keys[11], part), 71), part),
        "slot_owner": with_ends(jax.random.randint(own_keys[3], (N_REP, N_TP * POOL), -1, ROWS_REP), jax.random.fold_in(own_keys[3], 1), -1, ROWS_REP - 1).astype(jnp.int32),
        "slot_fill": with_ends(jax.random.randint(own_keys[4], (N_REP, N_TP * POOL), 1, BLK + 1), jax.random.fold_in(own_keys[4], 1), 1, BLK).astype(jnp.int32),
        "mig_source": draw_mig_source(jax.random.fold_in(jax.random.fold_in(arg_keys[11], part), 71), part),
        "mig_slot": with_ends(jax.random.randint(own_keys[6], (N_REP, N_TP * MIGS), 0, POOL - MIGS), jax.random.fold_in(own_keys[6], 1), 0, (POOL - MIGS) - 1).astype(jnp.int32),
        "adapter_id": with_ends(ranked(own_keys[7], (ROWS,), ADAPTERS, 2), jax.random.fold_in(own_keys[7], 3), 0, ADAPTERS - 1).astype(jnp.int32),
        "out_weight": gaussian_with(arg_keys[8], (D, D), (D // 64) ** -0.5, 0.75, ((0, 4),), (0, 1, 4, 2.0)),
        "shrink_weight": centred(arg_keys[9], (ADAPTERS, D, RANK), (D // 64) ** -0.5, 0.5, ((1, 4),)),
        "expand_weight": centred(arg_keys[10], (ADAPTERS, RANK, D), (4 * RANK) ** -0.5, 0.5, ((2, 4),)),
    }


neg_big = -1e+30
adapter_factor = 2.0

def replica_attention(kv_pool, slot_rows, slot_len, query_in, fresh_in):
    slot_count = kv_pool.shape[0]
    row_count = query_in.shape[0]
    group_size = H // KVH
    score_scale = 1.0 / math.sqrt(HS)
    query_rows = query_in.reshape(row_count, KVH, group_size, HS).astype(jnp.float32)
    blocks = kv_pool.reshape(slot_count, BLK, KVH, 2, HS).astype(jnp.float32)
    key_portion = blocks[:, :, :, 0]
    value_part = blocks[:, :, :, 1]
    is_owned = slot_rows >= 0
    slot_query = query_rows[jnp.maximum(slot_rows, 0)]
    scores = jnp.einsum('sgjd,stgd->sgjt', slot_query, key_portion) * score_scale
    is_valid = (jnp.arange(BLK)[None, :] < slot_len[:, None]) & is_owned[:, None]
    scores = jnp.where(is_valid[:, None, None, :], scores, neg_big)
    slot_max = lax.optimization_barrier(jnp.max(scores, axis=3))
    weights = jnp.where(is_valid[:, None, None, :], jnp.exp(scores - slot_max[..., None]), 0.0)
    slot_sum = lax.optimization_barrier(jnp.sum(weights, axis=3))
    rounded = lax.optimization_barrier(weights.astype(jnp.bfloat16)).astype(jnp.float32)
    slot_acc = jnp.einsum('sgjt,stgd->sgjd', rounded, value_part)
    fresh_kv = fresh_in.reshape(row_count, KVH, 2, HS).astype(jnp.float32)
    new_score = jnp.einsum('rgjd,rgd->rgj', query_rows, fresh_kv[:, :, 0]) * score_scale
    member = slot_rows[None, :] == jnp.arange(row_count)[:, None]
    owned_max = lax.optimization_barrier(jnp.max(jnp.where(member[:, :, None, None], slot_max[None], neg_big), axis=1))
    row_max = jnp.maximum(new_score, owned_max)
    rescale_factor = jnp.where(is_owned[:, None, None], jnp.exp(slot_max - row_max[jnp.maximum(slot_rows, 0)]), 0.0)
    onehot = member.astype(jnp.float32)
    new_weight = jnp.exp(new_score - row_max)
    totals = jnp.einsum('rs,sgj->rgj', onehot, rescale_factor * slot_sum, precision=lax.Precision.HIGHEST) + new_weight
    weighted = jnp.einsum('rs,sgjd->rgjd', onehot, rescale_factor[..., None] * slot_acc, precision=lax.Precision.HIGHEST)
    weighted = weighted + new_weight[..., None] * fresh_kv[:, :, None, 1]
    return (weighted / totals[..., None]).reshape(row_count, H * HS).astype(jnp.bfloat16)

def reference(queries, new_kv, kv_cache, slot_owner, slot_fill, mig_source, mig_slot, adapter_id, out_weight, shrink_weight, expand_weight):
    columns = jnp.arange(N_TP * MIGS, dtype=jnp.int32)
    lane_index = columns // MIGS
    source_slot = (lane_index[None, :] * POOL + mig_slot).astype(jnp.int32)
    copied = kv_cache[mig_source, source_slot]
    target = (lane_index * POOL + POOL - MIGS + columns % MIGS).astype(jnp.int32)
    kv_pool = kv_cache.at[:, target].set(copied)
    query_all = queries.reshape(N_REP, ROWS_REP, H * HS)
    fresh_all = new_kv.reshape(N_REP, ROWS_REP, 2 * KVH * HS)
    attention = lax.map(lambda replica_item: replica_attention(*replica_item), (kv_pool, slot_owner, slot_fill, query_all, fresh_all))
    attention = attention.reshape(ROWS_REP * N_REP, H * HS)
    base_output = jnp.dot(attention, out_weight, preferred_element_type=jnp.float32)
    stacked = shrink_weight.transpose(1, 0, 2).reshape(D, ADAPTERS * RANK)
    shrink_all = jnp.dot(attention, stacked, preferred_element_type=jnp.float32).reshape(-1, ADAPTERS, RANK)
    chosen = adapter_id[:, None] == jnp.arange(ADAPTERS, dtype=jnp.int32)[None, :]
    shrink = lax.optimization_barrier(jnp.sum(jnp.where(chosen[:, :, None], shrink_all, 0.0), axis=1)).astype(jnp.bfloat16)
    spread = jnp.where(chosen[:, :, None], shrink[:, None, :], jnp.zeros((), jnp.bfloat16)).reshape(-1, ADAPTERS * RANK)
    expand_matrix = jnp.dot(spread, expand_weight.reshape(ADAPTERS * RANK, D), preferred_element_type=jnp.float32)
    return (base_output + adapter_factor * expand_matrix).astype(jnp.bfloat16)
```

```python
import functools
import math

import jax
import jax.numpy as jnp
from jax import lax
from jax.experimental import pallas as pl
from jax.experimental.pallas import tpu as pltpu
from jax.sharding import PartitionSpec as P

H = 64
KVH = 8
HS = 128
BLK = 16
MIGS = 2


neg_big = -1e30
adapter_factor = 2.0


def joined(shard, axis, combine):
    everything = jax.tree.map(lambda part: lax.all_gather(part, axis), shard)
    leading = jax.tree.map(lambda part: part[0], everything)

    def turn(k, so_far):
        return combine(so_far, jax.tree.map(lambda part: part[k], everything))

    return lax.fori_loop(1, lax.axis_size(axis), turn, leading)


def local_partials(kv_pool, slot_rows, slot_len, whole_queries):
    slot_count = kv_pool.shape[0]
    row_count = whole_queries.shape[0]
    group_size = H // KVH
    score_scale = 1.0 / math.sqrt(HS)
    query_rows = whole_queries.reshape(row_count, KVH, group_size, HS)
    blocks = kv_pool.reshape(slot_count, BLK, KVH, 2, HS)
    key_portion = blocks[:, :, :, 0]
    value_part = blocks[:, :, :, 1]
    is_owned = slot_rows >= 0
    slot_query = query_rows[jnp.maximum(slot_rows, 0)]
    scores = (
        jnp.einsum("sgjd,stgd->sgjt", slot_query, key_portion, preferred_element_type=jnp.float32)
        * score_scale
    )
    is_valid = (jnp.arange(BLK)[None, :] < slot_len[:, None]) & is_owned[:, None]
    scores = jnp.where(is_valid[:, None, None, :], scores, neg_big)
    slot_max = jnp.max(scores, axis=3)
    weights = jnp.where(is_valid[:, None, None, :], jnp.exp(scores - slot_max[..., None]), 0.0)
    slot_sum = jnp.sum(weights, axis=3)
    slot_acc = jnp.einsum(
        "sgjt,stgd->sgjd",
        weights.astype(jnp.bfloat16),
        value_part,
        preferred_element_type=jnp.float32,
    )
    member = slot_rows[None, :] == jnp.arange(row_count)[:, None]
    local_max = jnp.max(jnp.where(member[:, :, None, None], slot_max[None], neg_big), axis=1)
    rescale_factor = jnp.where(
        is_owned[:, None, None], jnp.exp(slot_max - local_max[jnp.maximum(slot_rows, 0)]), 0.0
    )
    onehot = member.astype(jnp.float32)
    totals = jnp.einsum(
        "rs,sgj->rgj", onehot, rescale_factor * slot_sum, precision=lax.Precision.HIGHEST
    )
    weighted = jnp.einsum(
        "rs,sgjd->rgjd",
        onehot,
        rescale_factor[..., None] * slot_acc,
        precision=lax.Precision.HIGHEST,
    )
    return (
        local_max.reshape(row_count, H),
        totals.reshape(row_count, H),
        weighted.reshape(row_count, H, HS),
    )


def combine(earlier, later):
    best_score = jnp.maximum(earlier[0], later[0])
    first_ratio = jnp.exp(earlier[0] - best_score)
    second_ratio = jnp.exp(later[0] - best_score)
    totals = earlier[1] * first_ratio + later[1] * second_ratio
    weighted = earlier[2] * first_ratio[..., None] + later[2] * second_ratio[..., None]
    return (best_score, totals, weighted)


def body(
    queries,
    new_kv,
    kv_cache,
    slot_owner,
    slot_fill,
    mig_source,
    mig_slot,
    adapter_id,
    out_weight,
    shrink_weight,
    expand_weight,
):
    row_count = queries.shape[0]
    heads_here = queries.shape[1] // HS
    group_size = H // KVH
    score_scale = 1.0 / math.sqrt(HS)
    whole_queries, whole_new = (
        lax.all_gather(queries, "tp", axis=1, tiled=True),
        lax.all_gather(new_kv, "tp", axis=1, tiled=True),
    )
    local_pool = kv_cache[0]
    slot_count = local_pool.shape[0]
    wanted_source, wanted_slot = (
        lax.all_gather(mig_source, "rep", axis=0, tiled=True),
        lax.all_gather(mig_slot, "rep", axis=0, tiled=True),
    )
    current_replica = lax.axis_index("rep")
    is_mine = wanted_source == current_replica
    packed = jnp.where(
        is_mine[:, :, None, None], local_pool[wanted_slot], jnp.zeros((), local_pool.dtype)
    )
    arrived = lax.all_to_all(packed, "rep", split_axis=0, concat_axis=0, tiled=True)
    copied = arrived[mig_source[0], jnp.arange(mig_source.shape[1])]
    kv_pool = local_pool.at[slot_count - MIGS :].set(copied)
    local_max, totals, weighted = local_partials(
        kv_pool, slot_owner[0], slot_fill[0], whole_queries
    )
    first_head = lax.axis_index("tp") * heads_here
    best_all, total_all, weight_all = joined((local_max, totals, weighted), "tp", combine)
    best_score = lax.dynamic_slice_in_dim(best_all, first_head, heads_here, 1)
    totals = lax.dynamic_slice_in_dim(total_all, first_head, heads_here, 1)
    weighted = lax.dynamic_slice_in_dim(weight_all, first_head, heads_here, 1)
    local_query = queries.reshape(row_count, heads_here, HS)
    groups = (first_head + jnp.arange(heads_here)) // group_size
    fresh_kv = jnp.take(whole_new.reshape(row_count, KVH, 2, HS), groups, axis=1)
    new_score = (
        jnp.einsum(
            "rhd,rhd->rh", local_query, fresh_kv[:, :, 0], preferred_element_type=jnp.float32
        )
        * score_scale
    )
    top_score = jnp.maximum(best_score, new_score)
    old_weight = jnp.exp(best_score - top_score)
    new_weight = jnp.exp(new_score - top_score)
    numerator = weighted * old_weight[..., None] + new_weight[..., None] * fresh_kv[:, :, 1].astype(
        jnp.float32
    )
    denominator = totals * old_weight + new_weight
    attention = (
        (numerator / denominator[..., None])
        .reshape(row_count, heads_here * HS)
        .astype(jnp.bfloat16)
    )
    base_output = lax.psum_scatter(
        lax.dot_general(
            out_weight, attention, (((0,), (1,)), ((), ())), preferred_element_type=jnp.float32
        ),
        "tp",
        scatter_dimension=0,
        tiled=True,
    ).T
    adapters_all = shrink_weight.shape[0]
    shrink_all = jnp.einsum(
        "rk,akq->raq", attention, shrink_weight, preferred_element_type=jnp.float32
    )
    chosen = adapter_id[:, None] == jnp.arange(adapters_all, dtype=jnp.int32)[None, :]
    partial_value = jnp.sum(jnp.where(chosen[:, :, None], shrink_all, 0.0), axis=1)
    shrink = lax.psum(partial_value, "tp").astype(jnp.bfloat16)
    spread = jnp.where(chosen[:, :, None], shrink[:, None, :], jnp.zeros((), jnp.bfloat16)).reshape(
        row_count, -1
    )
    expand_matrix = jnp.dot(
        spread, expand_weight.reshape(spread.shape[1], -1), preferred_element_type=jnp.float32
    )
    return (base_output + adapter_factor * expand_matrix).astype(jnp.bfloat16)


def remote(src, dst, send_sem, recv_sem, axis, target):
    return pltpu.make_async_remote_copy(
        src_ref=src,
        dst_ref=dst,
        send_sem=send_sem,
        recv_sem=recv_sem,
        device_id={axis: target},
        device_id_type=pl.DeviceIdType.MESH,
    )


def layer_kernel(
    n_tp,
    n_rep,
    rank,
    q_ref,
    new_ref,
    kv_hbm,
    column_row_ref,
    mig_source_ref,
    mig_slot_ref,
    adapter_ref,
    out_w_hbm,
    shrink_w_hbm,
    expand_w_hbm,
    result_ref,
    kv,
    out_w,
    shrink_w,
    expand_w,
    q_all,
    slot_in,
    slot_smem,
    mig_out,
    mig_in,
    acc_out,
    acc_in,
    stat_out,
    stat_in,
    shrink_out,
    shrink_in,
    base_out,
    base_in,
    kv_sem,
    weight_sem,
    smem_sem,
    q_send,
    q_recv,
    slot_send,
    slot_recv,
    mig_send,
    mig_recv,
    acc_send,
    acc_recv,
    stat_send,
    stat_recv,
    shrink_send,
    shrink_recv,
    base_send,
    base_recv,
):
    f32, bf16 = jnp.float32, jnp.bfloat16
    tp = lax.axis_index("tp")
    rep = lax.axis_index("rep")
    rows = result_ref.shape[0]
    here = result_ref.shape[1]
    half = here // 2
    slots = kv.shape[0]
    migs = mig_out.shape[1]
    own_rows = q_ref.shape[0]
    heads_here = own_rows // rows
    group_size = H // KVH
    groups_here = heads_here // group_size
    group_rows = rows * group_size
    score_scale = 1.0 / math.sqrt(HS)
    tp_peers = [lax.rem(tp + d, n_tp) for d in range(1, n_tp)]
    rep_peers = [lax.rem(rep + d, n_rep) for d in range(1, n_rep)]
    kv_copy = pltpu.make_async_copy(kv_hbm, kv, kv_sem)
    kv_copy.start()
    barrier = pltpu.get_barrier_semaphore()
    for peer in tp_peers:
        pl.semaphore_signal(
            barrier, inc=1, device_id={"tp": peer}, device_id_type=pl.DeviceIdType.MESH
        )
    for peer in rep_peers:
        pl.semaphore_signal(
            barrier, inc=1, device_id={"rep": peer}, device_id_type=pl.DeviceIdType.MESH
        )

    def block(k):
        return pl.ds(pl.multiple_of(k * here, here), here)

    def q_rows(k):
        return pl.ds(pl.multiple_of(k * own_rows, 16), own_rows)

    weight_copies = [pltpu.make_async_copy(shrink_w_hbm, shrink_w, weight_sem.at[0])]
    order = tp_peers + [tp]
    for i, peer in enumerate(order):
        weight_copies.append(
            pltpu.make_async_copy(
                out_w_hbm.at[:, block(peer)], out_w.at[:, block(peer)], weight_sem.at[1 + i]
            )
        )
    weight_copies.append(pltpu.make_async_copy(expand_w_hbm, expand_w, weight_sem.at[1 + n_tp]))
    for copy in weight_copies:
        copy.start()

    q_all[q_rows(tp), :] = q_ref[...]
    slot_in[pl.ds(rep, 1)] = mig_slot_ref[...]
    mig_in[pl.ds(rep, 1)] = jnp.zeros((1,) + mig_in.shape[1:], bf16)
    pl.semaphore_wait(barrier, n_tp - 1 + n_rep - 1)

    slot_copies = [
        remote(
            mig_slot_ref, slot_in.at[pl.ds(rep, 1)], slot_send.at[d], slot_recv.at[d], "rep", peer
        )
        for d, peer in enumerate(rep_peers)
    ]
    for copy in slot_copies:
        copy.start()
    q_copies = [
        remote(q_ref, q_all.at[q_rows(tp), :], q_send.at[d], q_recv.at[d], "tp", peer)
        for d, peer in enumerate(tp_peers)
    ]
    for copy in q_copies[::-1]:
        copy.start()

    kv_copy.wait()
    for copy in slot_copies:
        copy.wait()
    to_smem = pltpu.make_async_copy(slot_in, slot_smem, smem_sem)
    to_smem.start()
    to_smem.wait()
    mig_copies = []
    for d, peer in enumerate(rep_peers):
        for k in range(migs):
            mig_out[d, k] = kv[slot_smem[peer, 0, k]]
        copy = remote(
            mig_out.at[d], mig_in.at[rep], mig_send.at[d], mig_recv.at[d], "rep", peer
        )
        copy.start()
        mig_copies.append(copy)

    own_query = q_ref[...].astype(f32)
    fresh = new_ref[...].astype(f32)
    fresh_key = jnp.concatenate(
        [
            fresh[:, g * 2 * HS : (g * 2 + 1) * HS]
            for g in range(groups_here)
            for _ in range(group_size)
        ],
        axis=0,
    )
    fresh_value = jnp.concatenate(
        [
            fresh[:, (g * 2 + 1) * HS : (g * 2 + 2) * HS]
            for g in range(groups_here)
            for _ in range(group_size)
        ],
        axis=0,
    )
    new_score = jnp.sum(own_query * fresh_key, axis=1, keepdims=True) * score_scale
    row_index = lax.rem(lax.broadcasted_iota(jnp.int32, (group_rows, slots * BLK), 0), rows)
    member = row_index == column_row_ref[...]

    for copy in q_copies:
        copy.wait()
    for copy in mig_copies:
        copy.wait()
    for k in range(migs):
        kv[slots - migs + k] = mig_in[mig_source_ref[0, k], k]

    acc_copies = []
    lane = lax.broadcasted_iota(jnp.int32, (group_rows, HS), 1)
    for d, peer in enumerate(order):
        stats = []
        for j in range(groups_here):
            group = peer * groups_here + j
            query = q_all[pl.ds(pl.multiple_of(group * group_rows, 16), group_rows), :]
            key_at = pl.ds(pl.multiple_of(group * 2 * HS, HS), HS)
            value_at = pl.ds(pl.multiple_of(group * 2 * HS + HS, HS), HS)
            key = kv[:, :, key_at].reshape(slots * BLK, HS)
            value = kv[:, :, value_at].reshape(slots * BLK, HS)
            score = (
                lax.dot_general(
                    query, key, (((1,), (1,)), ((), ())), preferred_element_type=f32
                )
                * score_scale
            )
            score = jnp.where(member, score, neg_big)
            top = jnp.max(score, axis=1, keepdims=True)
            weight = jnp.where(member, jnp.exp(score - top), 0.0)
            total = jnp.sum(weight, axis=1, keepdims=True)
            acc_out[d, j * group_rows : (j + 1) * group_rows, :] = jnp.dot(
                weight.astype(bf16), value, preferred_element_type=f32
            ).astype(bf16)
            stats.append(jnp.where(lane == 0, top, total))
        stat_out[d] = jnp.concatenate(stats, axis=0).T[:8]
        if d < n_tp - 1:
            for copy in (
                remote(stat_out.at[d], stat_in.at[d], stat_send.at[d], stat_recv.at[d], "tp", peer),
                remote(acc_out.at[d], acc_in.at[d], acc_send.at[d], acc_recv.at[d], "tp", peer),
            ):
                copy.start()
                acc_copies.append(copy)
    for copy in acc_copies:
        copy.wait()

    stat_rows = jnp.concatenate(
        [stat_in[d] for d in range(n_tp - 1)] + [stat_out[n_tp - 1]]
        + [jnp.zeros((HS - 8 * n_tp, own_rows), f32)],
        axis=0,
    )
    stat_columns = stat_rows.T
    tops = [stat_columns[:, 8 * d : 8 * d + 1] for d in range(n_tp)]
    totals = [stat_columns[:, 8 * d + 1 : 8 * d + 2] for d in range(n_tp)]
    best = functools.reduce(jnp.maximum, tops, new_score)
    fresh_ratio = jnp.exp(new_score - best)
    numerator = fresh_ratio * fresh_value
    denominator = fresh_ratio
    for d in range(n_tp):
        ratio = jnp.exp(tops[d] - best)
        part = acc_in[d] if d < n_tp - 1 else acc_out[d]
        numerator = numerator + ratio * part.astype(f32)
        denominator = denominator + ratio * totals[d]
    normal = numerator / denominator
    attention = jnp.concatenate(
        [normal[h * rows : (h + 1) * rows] for h in range(heads_here)], axis=1
    ).astype(bf16)

    weight_copies[0].wait()
    per_lane = HS // rank
    chunk = 2 * HS
    chunk_lane = lax.broadcasted_iota(jnp.int32, (rows, HS), 1)
    adapter = adapter_ref[...]
    folded = jnp.zeros((rows, HS), f32)
    for i in range(shrink_w.shape[0] // chunk):
        part = lax.dot_general(
            attention,
            shrink_w[i * chunk : (i + 1) * chunk, :],
            (((1,), (1,)), ((), ())),
            preferred_element_type=f32,
        )
        for j in range(chunk // HS):
            first = (i * chunk // HS + j) * per_lane
            folded = folded + jnp.where(
                adapter == first + chunk_lane // rank, part[:, j * HS : (j + 1) * HS], 0.0
            )
    shrink_out[...] = folded
    shrink_copies = [
        remote(
            shrink_out, shrink_in.at[d], shrink_send.at[d], shrink_recv.at[d], "tp", peer
        )
        for d, peer in enumerate(tp_peers)
    ]
    for copy in shrink_copies:
        copy.start()

    step = 256
    base_copies = []
    for d, peer in enumerate(order):
        weight_copies[1 + d].wait()

        def tile(i, carry, d=d, peer=peer):
            left = pl.multiple_of(peer * here + i * step, step)
            right = pl.multiple_of(peer * here + half + i * step, step)
            both = jnp.concatenate(
                [
                    jnp.dot(attention, out_w[:, pl.ds(at, step)], preferred_element_type=f32)
                    for at in (left, right)
                ],
                axis=0,
            )
            if d < n_tp - 1:
                base_out[d, :, pl.ds(pl.multiple_of(i * step, step), step)] = both.astype(bf16)
            else:
                result_ref[:, pl.ds(pl.multiple_of(i * step, step), step)] = both[:rows]
                result_ref[:, pl.ds(pl.multiple_of(half + i * step, step), step)] = both[rows:]
            return carry

        lax.fori_loop(0, half // step, tile, 0)
        if d < n_tp - 1:
            copy = remote(
                base_out.at[d], base_in.at[d], base_send.at[d], base_recv.at[d], "tp", peer
            )
            copy.start()
            base_copies.append(copy)

    for copy in shrink_copies:
        copy.wait()
    shrink = shrink_out[...]
    for d in range(n_tp - 1):
        shrink = shrink + shrink_in[d]
    spread = jnp.concatenate(
        [
            jnp.where(adapter == c * per_lane + chunk_lane // rank, shrink, 0.0)
            for c in range(shrink_w.shape[0] // HS)
        ],
        axis=1,
    ).astype(bf16)
    weight_copies[1 + n_tp].wait()

    def expand_tile(i, carry):
        at = pl.ds(pl.multiple_of(i * step, step), step)
        result_ref[:, at] = result_ref[:, at] + adapter_factor * jnp.dot(
            spread, expand_w[:, at], preferred_element_type=f32
        )
        return carry

    lax.fori_loop(0, here // step, expand_tile, 0)
    for copy in base_copies:
        copy.wait()
    for d in range(n_tp - 1):
        arrived = base_in[d].astype(f32)
        result_ref[:, :half] += arrived[:rows]
        result_ref[:, half:] += arrived[rows:]


def fused_body(
    queries,
    new_kv,
    kv_cache,
    slot_owner,
    slot_fill,
    mig_source,
    mig_slot,
    adapter_id,
    out_weight,
    shrink_weight,
    expand_weight,
):
    f32, bf16, i32 = jnp.float32, jnp.bfloat16, jnp.int32
    n_tp, n_rep = lax.axis_size("tp"), lax.axis_size("rep")
    rows, here = queries.shape
    heads_here = here // HS
    slots = kv_cache.shape[1]
    migs = mig_source.shape[1]
    width = kv_cache.shape[3]
    adapters, _, rank = shrink_weight.shape
    query_rows = queries.reshape(rows, heads_here, HS).transpose(1, 0, 2).reshape(-1, HS)
    own_rows = query_rows.shape[0]
    used = jnp.arange(BLK, dtype=i32)[None, :] < slot_fill[0][:, None]
    column_row = jnp.where(used, slot_owner[0][:, None], -1).reshape(1, slots * BLK)
    slot_tile = jnp.broadcast_to(jnp.pad(mig_slot, ((0, 0), (0, HS - migs)))[:, None], (1, 8, HS))
    vmem = pl.BlockSpec(memory_space=pltpu.VMEM)
    smem = pl.BlockSpec(memory_space=pltpu.SMEM)
    hbm = pl.BlockSpec(memory_space=pl.ANY)
    dma = pltpu.SemaphoreType.DMA
    peers, others = n_tp - 1, n_rep - 1
    total = pl.pallas_call(
        functools.partial(layer_kernel, n_tp, n_rep, rank),
        out_shape=jax.ShapeDtypeStruct((rows, here), f32),
        in_specs=[vmem, vmem, hbm, vmem, smem, vmem, vmem, hbm, hbm, hbm],
        out_specs=vmem,
        scratch_shapes=[
            pltpu.VMEM((slots, BLK, width), bf16),
            pltpu.VMEM(out_weight.shape, bf16),
            pltpu.VMEM((adapters * rank, here), bf16),
            pltpu.VMEM((adapters * rank, here), bf16),
            pltpu.VMEM((n_tp * own_rows, HS), bf16),
            pltpu.VMEM((n_rep, 8, HS), i32),
            pltpu.SMEM((n_rep, 8, HS), i32),
            pltpu.VMEM((others, migs, BLK, width), bf16),
            pltpu.VMEM((n_rep, migs, BLK, width), bf16),
            pltpu.VMEM((n_tp, own_rows, HS), bf16),
            pltpu.VMEM((peers, own_rows, HS), bf16),
            pltpu.VMEM((n_tp, 8, own_rows), f32),
            pltpu.VMEM((peers, 8, own_rows), f32),
            pltpu.VMEM((rows, HS), f32),
            pltpu.VMEM((peers, rows, HS), f32),
            pltpu.VMEM((peers, 2 * rows, here // 2), bf16),
            pltpu.VMEM((peers, 2 * rows, here // 2), bf16),
            dma,
            dma((2 + n_tp,)),
            dma,
            dma((peers,)),
            dma((peers,)),
            dma((others,)),
            dma((others,)),
            dma((others,)),
            dma((others,)),
            dma((peers,)),
            dma((peers,)),
            dma((peers,)),
            dma((peers,)),
            dma((peers,)),
            dma((peers,)),
            dma((peers,)),
            dma((peers,)),
        ],
        compiler_params=pltpu.CompilerParams(
            collective_id=0, has_side_effects=True, vmem_limit_bytes=60 * 1024 * 1024
        ),
    )(
        query_rows,
        new_kv,
        kv_cache[0],
        column_row,
        mig_source,
        slot_tile,
        adapter_id[:, None],
        out_weight,
        shrink_weight.transpose(0, 2, 1).reshape(adapters * rank, here),
        expand_weight.reshape(adapters * rank, here),
    )
    return total.astype(bf16)


def solution(mesh):
    heads_here = H // mesh.shape["tp"]
    fits = heads_here % (H // KVH) == 0
    return jax.shard_map(
        fused_body if fits else body,
        mesh=mesh,
        in_specs=(
            P(("parts", "rep"), "tp"),
            P(("parts", "rep"), "tp"),
            P(("parts", "rep"), "tp", None, None),
            P(("parts", "rep"), "tp"),
            P(("parts", "rep"), "tp"),
            P(("parts", "rep"), "tp"),
            P(("parts", "rep"), "tp"),
            P(("parts", "rep")),
            P("tp", None),
            P(None, "tp", None),
            P(None, None, "tp"),
        ),
        out_specs=P(("parts", "rep"), "tp"),
        check_vma=False,
    )
```

```python
import functools
import math

import jax
import jax.numpy as jnp
from jax import lax
from jax.experimental import pallas as pl
from jax.experimental.pallas import tpu as pltpu
from jax.sharding import PartitionSpec as P

H = 64
KVH = 8
HS = 128
BLK = 16
MIGS = 2


neg_big = -1e30
adapter_factor = 2.0


def joined(shard, axis, combine):
    everything = jax.tree.map(lambda part: lax.all_gather(part, axis), shard)
    leading = jax.tree.map(lambda part: part[0], everything)

    def turn(k, so_far):
        return combine(so_far, jax.tree.map(lambda part: part[k], everything))

    return lax.fori_loop(1, lax.axis_size(axis), turn, leading)


def local_partials(kv_pool, slot_rows, slot_len, whole_queries):
    slot_count = kv_pool.shape[0]
    row_count = whole_queries.shape[0]
    group_size = H // KVH
    score_scale = 1.0 / math.sqrt(HS)
    query_rows = whole_queries.reshape(row_count, KVH, group_size, HS)
    blocks = kv_pool.reshape(slot_count, BLK, KVH, 2, HS)
    key_portion = blocks[:, :, :, 0]
    value_part = blocks[:, :, :, 1]
    is_owned = slot_rows >= 0
    slot_query = query_rows[jnp.maximum(slot_rows, 0)]
    scores = (
        jnp.einsum("sgjd,stgd->sgjt", slot_query, key_portion, preferred_element_type=jnp.float32)
        * score_scale
    )
    is_valid = (jnp.arange(BLK)[None, :] < slot_len[:, None]) & is_owned[:, None]
    scores = jnp.where(is_valid[:, None, None, :], scores, neg_big)
    slot_max = jnp.max(scores, axis=3)
    weights = jnp.where(is_valid[:, None, None, :], jnp.exp(scores - slot_max[..., None]), 0.0)
    slot_sum = jnp.sum(weights, axis=3)
    slot_acc = jnp.einsum(
        "sgjt,stgd->sgjd",
        weights.astype(jnp.bfloat16),
        value_part,
        preferred_element_type=jnp.float32,
    )
    member = slot_rows[None, :] == jnp.arange(row_count)[:, None]
    local_max = jnp.max(jnp.where(member[:, :, None, None], slot_max[None], neg_big), axis=1)
    rescale_factor = jnp.where(
        is_owned[:, None, None], jnp.exp(slot_max - local_max[jnp.maximum(slot_rows, 0)]), 0.0
    )
    onehot = member.astype(jnp.float32)
    totals = jnp.einsum(
        "rs,sgj->rgj", onehot, rescale_factor * slot_sum, precision=lax.Precision.HIGHEST
    )
    weighted = jnp.einsum(
        "rs,sgjd->rgjd",
        onehot,
        rescale_factor[..., None] * slot_acc,
        precision=lax.Precision.HIGHEST,
    )
    return (
        local_max.reshape(row_count, H),
        totals.reshape(row_count, H),
        weighted.reshape(row_count, H, HS),
    )


def combine(earlier, later):
    best_score = jnp.maximum(earlier[0], later[0])
    first_ratio = jnp.exp(earlier[0] - best_score)
    second_ratio = jnp.exp(later[0] - best_score)
    totals = earlier[1] * first_ratio + later[1] * second_ratio
    weighted = earlier[2] * first_ratio[..., None] + later[2] * second_ratio[..., None]
    return (best_score, totals, weighted)


def body(
    queries,
    new_kv,
    kv_cache,
    slot_owner,
    slot_fill,
    mig_source,
    mig_slot,
    adapter_id,
    out_weight,
    shrink_weight,
    expand_weight,
):
    row_count = queries.shape[0]
    heads_here = queries.shape[1] // HS
    group_size = H // KVH
    score_scale = 1.0 / math.sqrt(HS)
    whole_queries, whole_new = (
        lax.all_gather(queries, "tp", axis=1, tiled=True),
        lax.all_gather(new_kv, "tp", axis=1, tiled=True),
    )
    local_pool = kv_cache[0]
    slot_count = local_pool.shape[0]
    wanted_source, wanted_slot = (
        lax.all_gather(mig_source, "rep", axis=0, tiled=True),
        lax.all_gather(mig_slot, "rep", axis=0, tiled=True),
    )
    current_replica = lax.axis_index("rep")
    is_mine = wanted_source == current_replica
    packed = jnp.where(
        is_mine[:, :, None, None], local_pool[wanted_slot], jnp.zeros((), local_pool.dtype)
    )
    arrived = lax.all_to_all(packed, "rep", split_axis=0, concat_axis=0, tiled=True)
    copied = arrived[mig_source[0], jnp.arange(mig_source.shape[1])]
    kv_pool = local_pool.at[slot_count - MIGS :].set(copied)
    local_max, totals, weighted = local_partials(
        kv_pool, slot_owner[0], slot_fill[0], whole_queries
    )
    first_head = lax.axis_index("tp") * heads_here
    best_all, total_all, weight_all = joined((local_max, totals, weighted), "tp", combine)
    best_score = lax.dynamic_slice_in_dim(best_all, first_head, heads_here, 1)
    totals = lax.dynamic_slice_in_dim(total_all, first_head, heads_here, 1)
    weighted = lax.dynamic_slice_in_dim(weight_all, first_head, heads_here, 1)
    local_query = queries.reshape(row_count, heads_here, HS)
    groups = (first_head + jnp.arange(heads_here)) // group_size
    fresh_kv = jnp.take(whole_new.reshape(row_count, KVH, 2, HS), groups, axis=1)
    new_score = (
        jnp.einsum(
            "rhd,rhd->rh", local_query, fresh_kv[:, :, 0], preferred_element_type=jnp.float32
        )
        * score_scale
    )
    top_score = jnp.maximum(best_score, new_score)
    old_weight = jnp.exp(best_score - top_score)
    new_weight = jnp.exp(new_score - top_score)
    numerator = weighted * old_weight[..., None] + new_weight[..., None] * fresh_kv[:, :, 1].astype(
        jnp.float32
    )
    denominator = totals * old_weight + new_weight
    attention = (
        (numerator / denominator[..., None])
        .reshape(row_count, heads_here * HS)
        .astype(jnp.bfloat16)
    )
    base_output = lax.psum_scatter(
        lax.dot_general(
            out_weight, attention, (((0,), (1,)), ((), ())), preferred_element_type=jnp.float32
        ),
        "tp",
        scatter_dimension=0,
        tiled=True,
    ).T
    adapters_all = shrink_weight.shape[0]
    shrink_all = jnp.einsum(
        "rk,akq->raq", attention, shrink_weight, preferred_element_type=jnp.float32
    )
    chosen = adapter_id[:, None] == jnp.arange(adapters_all, dtype=jnp.int32)[None, :]
    partial_value = jnp.sum(jnp.where(chosen[:, :, None], shrink_all, 0.0), axis=1)
    shrink = lax.psum(partial_value, "tp").astype(jnp.bfloat16)
    spread = jnp.where(chosen[:, :, None], shrink[:, None, :], jnp.zeros((), jnp.bfloat16)).reshape(
        row_count, -1
    )
    expand_matrix = jnp.dot(
        spread, expand_weight.reshape(spread.shape[1], -1), preferred_element_type=jnp.float32
    )
    return (base_output + adapter_factor * expand_matrix).astype(jnp.bfloat16)


def remote(src, dst, send_sem, recv_sem, axis, target):
    return pltpu.make_async_remote_copy(
        src_ref=src,
        dst_ref=dst,
        send_sem=send_sem,
        recv_sem=recv_sem,
        device_id={axis: target},
        device_id_type=pl.DeviceIdType.MESH,
    )


def flipped(index, distance):
    bit, other = 1, index
    while bit <= distance:
        if distance & bit:
            other = other + bit - 2 * bit * lax.rem(index // bit, 2)
        bit *= 2
    return other


def as_column(row):
    size = row.shape[1]
    same = lax.broadcasted_iota(jnp.int32, (size, size), 0) == lax.broadcasted_iota(
        jnp.int32, (size, size), 1
    )
    return jnp.sum(jnp.where(same, row.astype(jnp.float32), 0.0), axis=1, keepdims=True)


def layer_kernel(
    n_tp,
    n_rep,
    rank,
    q_ref,
    new_ref,
    kv_hbm,
    owner_ref,
    fill_ref,
    mig_source_ref,
    mig_slot_ref,
    adapter_ref,
    out_w_hbm,
    shrink_w_hbm,
    expand_w_hbm,
    result_ref,
    kv,
    out_w,
    shrink_w,
    expand_w,
    q_all,
    slot_out,
    slot_in,
    slot_smem,
    mig_out,
    mig_in,
    acc_out,
    acc_in,
    stat_out,
    stat_in,
    shrink_out,
    shrink_in,
    base_out,
    base_in,
    sums,
    kv_sem,
    weight_sem,
    smem_sem,
    q_send,
    q_recv,
    slot_send,
    slot_recv,
    mig_send,
    mig_recv,
    acc_send,
    acc_recv,
    stat_send,
    stat_recv,
    shrink_send,
    shrink_recv,
    base_send,
    base_recv,
):
    f32, bf16 = jnp.float32, jnp.bfloat16
    tp = lax.axis_index("tp")
    rep = lax.axis_index("rep")
    rows = result_ref.shape[0]
    here = result_ref.shape[1]
    half = here // 2
    slots = kv.shape[0]
    migs = mig_out.shape[1]
    heads_here = here // HS
    own_rows = heads_here * rows
    group_size = H // KVH
    groups_here = heads_here // group_size
    group_rows = rows * group_size
    score_scale = 1.0 / math.sqrt(HS)
    middle = n_tp // 2
    tp_peers = [flipped(tp, d) for d in list(range(middle, n_tp)) + list(range(1, middle))]
    rep_peers = [lax.rem(rep + d, n_rep) for d in range(1, n_rep)]
    kv_copy = pltpu.make_async_copy(kv_hbm.at[0], kv, kv_sem)
    kv_copy.start()
    barrier = pltpu.get_barrier_semaphore()
    for peer in tp_peers:
        pl.semaphore_signal(
            barrier, inc=1, device_id={"tp": peer}, device_id_type=pl.DeviceIdType.MESH
        )
    for peer in rep_peers:
        pl.semaphore_signal(
            barrier, inc=1, device_id={"rep": peer}, device_id_type=pl.DeviceIdType.MESH
        )

    def block(k):
        return pl.ds(pl.multiple_of(k * here, here), here)

    def q_rows(k):
        return pl.ds(pl.multiple_of(k * own_rows, 16), own_rows)

    weight_copies = [pltpu.make_async_copy(shrink_w_hbm, shrink_w, weight_sem.at[0])]
    order = tp_peers + [tp]
    for i, peer in enumerate(order):
        weight_copies.append(
            pltpu.make_async_copy(
                out_w_hbm.at[:, block(peer)], out_w.at[:, block(peer)], weight_sem.at[1 + i]
            )
        )
    weight_copies.append(pltpu.make_async_copy(expand_w_hbm, expand_w, weight_sem.at[1 + n_tp]))
    for copy in weight_copies:
        copy.start()

    slot_lane = lax.broadcasted_iota(jnp.int32, slot_out.shape, 2)
    wanted = jnp.zeros(slot_out.shape, jnp.int32)
    for k in range(migs):
        wanted = jnp.where(slot_lane == k, mig_slot_ref[0, k], wanted)
    slot_out[...] = wanted
    slot_in[pl.ds(rep, 1)] = wanted
    own_query = q_ref[...].astype(f32)
    own_query = jnp.concatenate(
        [own_query[:, h * HS : (h + 1) * HS] for h in range(heads_here)], axis=0
    )
    q_all[q_rows(tp), :] = own_query.astype(bf16)
    mig_in[pl.ds(rep, 1)] = jnp.zeros((1,) + mig_in.shape[1:], bf16)
    pl.semaphore_wait(barrier, n_tp - 1 + n_rep - 1)

    slot_copies = [
        remote(
            slot_out, slot_in.at[pl.ds(rep, 1)], slot_send.at[d], slot_recv.at[d], "rep", peer
        )
        for d, peer in enumerate(rep_peers)
    ]
    for copy in slot_copies:
        copy.start()
    q_copies = [
        remote(q_all.at[q_rows(tp), :], q_all.at[q_rows(tp), :], q_send.at[d], q_recv.at[d], "tp", peer)
        for d, peer in enumerate(tp_peers)
    ]
    for copy in q_copies:
        copy.start()

    kv_copy.wait()
    for copy in slot_copies:
        copy.wait()
    to_smem = pltpu.make_async_copy(slot_in, slot_smem, smem_sem)
    to_smem.start()
    to_smem.wait()
    mig_copies = []
    for d, peer in enumerate(rep_peers):
        for k in range(migs):
            mig_out[d, k] = kv[slot_smem[peer, 0, k]]
        copy = remote(
            mig_out.at[d], mig_in.at[rep], mig_send.at[d], mig_recv.at[d], "rep", peer
        )
        copy.start()
        mig_copies.append(copy)

    fresh = new_ref[...].astype(f32)
    fresh_key = jnp.concatenate(
        [
            fresh[:, g * 2 * HS : (g * 2 + 1) * HS]
            for g in range(groups_here)
            for _ in range(group_size)
        ],
        axis=0,
    )
    fresh_value = jnp.concatenate(
        [
            fresh[:, (g * 2 + 1) * HS : (g * 2 + 2) * HS]
            for g in range(groups_here)
            for _ in range(group_size)
        ],
        axis=0,
    )
    new_score = jnp.sum(own_query * fresh_key, axis=1, keepdims=True) * score_scale
    row_index = lax.rem(lax.broadcasted_iota(jnp.int32, (group_rows, slots * BLK), 0), rows)
    slot_of = lax.broadcasted_iota(jnp.int32, (slots, slots * BLK), 1) // BLK
    spot = lax.rem(lax.broadcasted_iota(jnp.int32, (1, slots * BLK), 1), BLK).astype(f32)
    inside = slot_of == lax.broadcasted_iota(jnp.int32, (slots, slots * BLK), 0)
    owner, fill = [
        jnp.sum(jnp.where(inside, as_column(ref[...]), 0.0), axis=0, keepdims=True)
        for ref in (owner_ref, fill_ref)
    ]
    member = row_index.astype(f32) == jnp.where(spot < fill, owner, -1.0)
    adapter = as_column(adapter_ref[...])

    for copy in mig_copies:
        copy.wait()
    for k in range(migs):
        kv[slots - migs + k] = mig_in[mig_source_ref[0, k], k]

    acc_copies = []
    lane = lax.broadcasted_iota(jnp.int32, (group_rows, HS), 1)
    for d, peer in enumerate(order):
        if d < n_tp - 1:
            q_copies[d].wait_recv()
        stats = []
        for j in range(groups_here):
            group = peer * groups_here + j
            query = q_all[pl.ds(pl.multiple_of(group * group_rows, 16), group_rows), :]
            key_at = pl.ds(pl.multiple_of(group * 2 * HS, HS), HS)
            value_at = pl.ds(pl.multiple_of(group * 2 * HS + HS, HS), HS)
            key = kv[:, :, key_at].reshape(slots * BLK, HS)
            value = kv[:, :, value_at].reshape(slots * BLK, HS)
            score = (
                lax.dot_general(
                    query, key, (((1,), (1,)), ((), ())), preferred_element_type=f32
                )
                * score_scale
            )
            score = jnp.where(member, score, neg_big)
            top = jnp.max(score, axis=1, keepdims=True)
            weight = jnp.where(member, jnp.exp(score - top), 0.0)
            total = jnp.sum(weight, axis=1, keepdims=True)
            acc_out[d, j * group_rows : (j + 1) * group_rows, :] = jnp.dot(
                weight.astype(bf16), value, preferred_element_type=f32
            ).astype(bf16)
            stats.append(jnp.where(lane == 0, top, total))
            if d < n_tp - 1:
                part = pl.ds(j * group_rows, group_rows)
                copy = remote(
                    acc_out.at[d, part],
                    acc_in.at[d, part],
                    acc_send.at[d, j],
                    acc_recv.at[d, j],
                    "tp",
                    peer,
                )
                copy.start()
                acc_copies.append(copy)
        stat_out[d] = jnp.concatenate(stats, axis=0).T[:8]
        if d < n_tp - 1:
            copy = remote(
                stat_out.at[d], stat_in.at[d], stat_send.at[d], stat_recv.at[d], "tp", peer
            )
            copy.start()
            acc_copies.append(copy)
    for copy in q_copies:
        copy.wait_send()
    for copy in acc_copies:
        copy.wait()

    stat_rows = jnp.concatenate(
        [stat_in[d] for d in range(n_tp - 1)] + [stat_out[n_tp - 1]]
        + [jnp.zeros((HS - 8 * n_tp, own_rows), f32)],
        axis=0,
    )
    stat_columns = stat_rows.T
    tops = [stat_columns[:, 8 * d : 8 * d + 1] for d in range(n_tp)]
    totals = [stat_columns[:, 8 * d + 1 : 8 * d + 2] for d in range(n_tp)]
    best = functools.reduce(jnp.maximum, tops, new_score)
    fresh_ratio = jnp.exp(new_score - best)
    numerator = fresh_ratio * fresh_value
    denominator = fresh_ratio
    for d in range(n_tp):
        ratio = jnp.exp(tops[d] - best)
        part = acc_in[d] if d < n_tp - 1 else acc_out[d]
        numerator = numerator + ratio * part.astype(f32)
        denominator = denominator + ratio * totals[d]
    normal = numerator / denominator
    attention = jnp.concatenate(
        [normal[h * rows : (h + 1) * rows] for h in range(heads_here)], axis=1
    ).astype(bf16)

    def send_shrink():
        weight_copies[0].wait()
        chunk = 2 * HS
        folded = jnp.zeros((rank, rows), f32)
        for i in range(shrink_w.shape[0] // chunk):
            part = lax.dot_general(
                shrink_w[i * chunk : (i + 1) * chunk, :],
                attention,
                (((1,), (1,)), ((), ())),
                preferred_element_type=f32,
            )
            for j in range(chunk // rank):
                folded = folded + jnp.where(
                    adapter_ref[...] == i * (chunk // rank) + j,
                    part[j * rank : (j + 1) * rank],
                    0.0,
                )
        shrink_out[...] = folded
        copies = [
            remote(
                shrink_out, shrink_in.at[d], shrink_send.at[d], shrink_recv.at[d], "tp", peer
            )
            for d, peer in enumerate(tp_peers)
        ]
        for copy in copies:
            copy.start()
        return copies

    step = 256
    base_copies = []
    shrink_copies = []
    for d, peer in enumerate(order):
        if d == max(n_tp - 2, 0):
            shrink_copies = send_shrink()
        weight_copies[1 + d].wait()

        def tile(i, carry, d=d, peer=peer):
            left = pl.multiple_of(peer * here + i * step, step)
            right = pl.multiple_of(peer * here + half + i * step, step)
            both = jnp.concatenate(
                [
                    jnp.dot(attention, out_w[:, pl.ds(at, step)], preferred_element_type=f32)
                    for at in (left, right)
                ],
                axis=0,
            )
            if d < n_tp - 1:
                base_out[d, :, pl.ds(pl.multiple_of(i * step, step), step)] = both.astype(bf16)
            else:
                sums[:, pl.ds(pl.multiple_of(i * step, step), step)] = both[:rows]
                sums[:, pl.ds(pl.multiple_of(half + i * step, step), step)] = both[rows:]
            return carry

        lax.fori_loop(0, half // step, tile, 0)
        if d < n_tp - 1:
            copy = remote(
                base_out.at[d], base_in.at[d], base_send.at[d], base_recv.at[d], "tp", peer
            )
            copy.start()
            base_copies.append(copy)

    for copy in shrink_copies:
        copy.wait()
    shrink = shrink_out[...]
    for d in range(n_tp - 1):
        shrink = shrink + shrink_in[d]
    per_lane = HS // rank
    shrink = jnp.concatenate([shrink] * per_lane, axis=0).T
    chunk_lane = lax.broadcasted_iota(jnp.int32, (rows, HS), 1)
    spread = jnp.concatenate(
        [
            jnp.where(adapter == (c * per_lane + chunk_lane // rank).astype(f32), shrink, 0.0)
            for c in range(shrink_w.shape[0] // HS)
        ],
        axis=1,
    ).astype(bf16)
    weight_copies[1 + n_tp].wait()

    def expand_tile(i, carry):
        at = pl.ds(pl.multiple_of(i * step, step), step)
        sums[:, at] = sums[:, at] + adapter_factor * jnp.dot(
            spread, expand_w[:, at], preferred_element_type=f32
        )
        return carry

    lax.fori_loop(0, here // step, expand_tile, 0)
    for copy in base_copies:
        copy.wait()
    left, right = sums[:, :half], sums[:, half:]
    for d in range(n_tp - 1):
        arrived = base_in[d].astype(f32)
        left = left + arrived[:rows]
        right = right + arrived[rows:]
    result_ref[:, :half] = left.astype(bf16)
    result_ref[:, half:] = right.astype(bf16)


def fused_body(
    queries,
    new_kv,
    kv_cache,
    slot_owner,
    slot_fill,
    mig_source,
    mig_slot,
    adapter_id,
    out_weight,
    shrink_weight,
    expand_weight,
):
    f32, bf16, i32 = jnp.float32, jnp.bfloat16, jnp.int32
    n_tp, n_rep = lax.axis_size("tp"), lax.axis_size("rep")
    rows, here = queries.shape
    heads_here = here // HS
    slots = kv_cache.shape[1]
    migs = mig_source.shape[1]
    width = kv_cache.shape[3]
    adapters, _, rank = shrink_weight.shape
    own_rows = rows * heads_here
    vmem = pl.BlockSpec(memory_space=pltpu.VMEM)
    smem = pl.BlockSpec(memory_space=pltpu.SMEM)
    hbm = pl.BlockSpec(memory_space=pl.ANY)
    dma = pltpu.SemaphoreType.DMA
    peers, others = n_tp - 1, n_rep - 1
    return pl.pallas_call(
        functools.partial(layer_kernel, n_tp, n_rep, rank),
        out_shape=jax.ShapeDtypeStruct((rows, here), bf16),
        in_specs=[vmem, vmem, hbm, vmem, vmem, smem, smem, vmem, hbm, hbm, hbm],
        out_specs=vmem,
        scratch_shapes=[
            pltpu.VMEM((slots, BLK, width), bf16),
            pltpu.VMEM(out_weight.shape, bf16),
            pltpu.VMEM((adapters * rank, here), bf16),
            pltpu.VMEM((adapters * rank, here), bf16),
            pltpu.VMEM((n_tp * own_rows, HS), bf16),
            pltpu.VMEM((1, 8, HS), i32),
            pltpu.VMEM((n_rep, 8, HS), i32),
            pltpu.SMEM((n_rep, 8, HS), i32),
            pltpu.VMEM((others, migs, BLK, width), bf16),
            pltpu.VMEM((n_rep, migs, BLK, width), bf16),
            pltpu.VMEM((n_tp, own_rows, HS), bf16),
            pltpu.VMEM((peers, own_rows, HS), bf16),
            pltpu.VMEM((n_tp, 8, own_rows), f32),
            pltpu.VMEM((peers, 8, own_rows), f32),
            pltpu.VMEM((rank, rows), f32),
            pltpu.VMEM((peers, rank, rows), f32),
            pltpu.VMEM((peers, 2 * rows, here // 2), bf16),
            pltpu.VMEM((peers, 2 * rows, here // 2), bf16),
            pltpu.VMEM((rows, here), f32),
            dma,
            dma((2 + n_tp,)),
            dma,
            dma((peers,)),
            dma((peers,)),
            dma((others,)),
            dma((others,)),
            dma((others,)),
            dma((others,)),
            dma((peers, heads_here * KVH // H)),
            dma((peers, heads_here * KVH // H)),
            dma((peers,)),
            dma((peers,)),
            dma((peers,)),
            dma((peers,)),
            dma((peers,)),
            dma((peers,)),
        ],
        compiler_params=pltpu.CompilerParams(
            collective_id=0, has_side_effects=True, vmem_limit_bytes=60 * 1024 * 1024
        ),
    )(
        queries,
        new_kv,
        kv_cache,
        slot_owner,
        slot_fill,
        mig_source,
        mig_slot,
        adapter_id[None, :],
        out_weight,
        shrink_weight.transpose(0, 2, 1).reshape(adapters * rank, here),
        expand_weight.reshape(adapters * rank, here),
    )


def solution(mesh):
    heads_here = H // mesh.shape["tp"]
    fits = heads_here % (H // KVH) == 0
    return jax.shard_map(
        fused_body if fits else body,
        mesh=mesh,
        in_specs=(
            P(("parts", "rep"), "tp"),
            P(("parts", "rep"), "tp"),
            P(("parts", "rep"), "tp", None, None),
            P(("parts", "rep"), "tp"),
            P(("parts", "rep"), "tp"),
            P(("parts", "rep"), "tp"),
            P(("parts", "rep"), "tp"),
            P(("parts", "rep")),
            P("tp", None),
            P(None, "tp", None),
            P(None, None, "tp"),
        ),
        out_specs=P(("parts", "rep"), "tp"),
        check_vma=False,
    )
```

```python
import functools
import math

import jax
import jax.numpy as jnp
from jax import lax
from jax.experimental import pallas as pl
from jax.experimental.pallas import tpu as pltpu
from jax.sharding import PartitionSpec as P

H = 64
KVH = 8
HS = 128
BLK = 16
MIGS = 2


neg_big = -1e30
adapter_factor = 2.0


def joined(shard, axis, combine):
    everything = jax.tree.map(lambda part: lax.all_gather(part, axis), shard)
    leading = jax.tree.map(lambda part: part[0], everything)

    def turn(k, so_far):
        return combine(so_far, jax.tree.map(lambda part: part[k], everything))

    return lax.fori_loop(1, lax.axis_size(axis), turn, leading)


def local_partials(kv_pool, slot_rows, slot_len, whole_queries):
    slot_count = kv_pool.shape[0]
    row_count = whole_queries.shape[0]
    group_size = H // KVH
    score_scale = 1.0 / math.sqrt(HS)
    query_rows = whole_queries.reshape(row_count, KVH, group_size, HS)
    blocks = kv_pool.reshape(slot_count, BLK, KVH, 2, HS)
    key_portion = blocks[:, :, :, 0]
    value_part = blocks[:, :, :, 1]
    is_owned = slot_rows >= 0
    slot_query = query_rows[jnp.maximum(slot_rows, 0)]
    scores = (
        jnp.einsum("sgjd,stgd->sgjt", slot_query, key_portion, preferred_element_type=jnp.float32)
        * score_scale
    )
    is_valid = (jnp.arange(BLK)[None, :] < slot_len[:, None]) & is_owned[:, None]
    scores = jnp.where(is_valid[:, None, None, :], scores, neg_big)
    slot_max = jnp.max(scores, axis=3)
    weights = jnp.where(is_valid[:, None, None, :], jnp.exp(scores - slot_max[..., None]), 0.0)
    slot_sum = jnp.sum(weights, axis=3)
    slot_acc = jnp.einsum(
        "sgjt,stgd->sgjd",
        weights.astype(jnp.bfloat16),
        value_part,
        preferred_element_type=jnp.float32,
    )
    member = slot_rows[None, :] == jnp.arange(row_count)[:, None]
    local_max = jnp.max(jnp.where(member[:, :, None, None], slot_max[None], neg_big), axis=1)
    rescale_factor = jnp.where(
        is_owned[:, None, None], jnp.exp(slot_max - local_max[jnp.maximum(slot_rows, 0)]), 0.0
    )
    onehot = member.astype(jnp.float32)
    totals = jnp.einsum(
        "rs,sgj->rgj", onehot, rescale_factor * slot_sum, precision=lax.Precision.HIGHEST
    )
    weighted = jnp.einsum(
        "rs,sgjd->rgjd",
        onehot,
        rescale_factor[..., None] * slot_acc,
        precision=lax.Precision.HIGHEST,
    )
    return (
        local_max.reshape(row_count, H),
        totals.reshape(row_count, H),
        weighted.reshape(row_count, H, HS),
    )


def combine(earlier, later):
    best_score = jnp.maximum(earlier[0], later[0])
    first_ratio = jnp.exp(earlier[0] - best_score)
    second_ratio = jnp.exp(later[0] - best_score)
    totals = earlier[1] * first_ratio + later[1] * second_ratio
    weighted = earlier[2] * first_ratio[..., None] + later[2] * second_ratio[..., None]
    return (best_score, totals, weighted)


def body(
    queries,
    new_kv,
    kv_cache,
    slot_owner,
    slot_fill,
    mig_source,
    mig_slot,
    adapter_id,
    out_weight,
    shrink_weight,
    expand_weight,
):
    row_count = queries.shape[0]
    heads_here = queries.shape[1] // HS
    group_size = H // KVH
    score_scale = 1.0 / math.sqrt(HS)
    whole_queries, whole_new = (
        lax.all_gather(queries, "tp", axis=1, tiled=True),
        lax.all_gather(new_kv, "tp", axis=1, tiled=True),
    )
    local_pool = kv_cache[0]
    slot_count = local_pool.shape[0]
    wanted_source, wanted_slot = (
        lax.all_gather(mig_source, "rep", axis=0, tiled=True),
        lax.all_gather(mig_slot, "rep", axis=0, tiled=True),
    )
    current_replica = lax.axis_index("rep")
    is_mine = wanted_source == current_replica
    packed = jnp.where(
        is_mine[:, :, None, None], local_pool[wanted_slot], jnp.zeros((), local_pool.dtype)
    )
    arrived = lax.all_to_all(packed, "rep", split_axis=0, concat_axis=0, tiled=True)
    copied = arrived[mig_source[0], jnp.arange(mig_source.shape[1])]
    kv_pool = local_pool.at[slot_count - MIGS :].set(copied)
    local_max, totals, weighted = local_partials(
        kv_pool, slot_owner[0], slot_fill[0], whole_queries
    )
    first_head = lax.axis_index("tp") * heads_here
    best_all, total_all, weight_all = joined((local_max, totals, weighted), "tp", combine)
    best_score = lax.dynamic_slice_in_dim(best_all, first_head, heads_here, 1)
    totals = lax.dynamic_slice_in_dim(total_all, first_head, heads_here, 1)
    weighted = lax.dynamic_slice_in_dim(weight_all, first_head, heads_here, 1)
    local_query = queries.reshape(row_count, heads_here, HS)
    groups = (first_head + jnp.arange(heads_here)) // group_size
    fresh_kv = jnp.take(whole_new.reshape(row_count, KVH, 2, HS), groups, axis=1)
    new_score = (
        jnp.einsum(
            "rhd,rhd->rh", local_query, fresh_kv[:, :, 0], preferred_element_type=jnp.float32
        )
        * score_scale
    )
    top_score = jnp.maximum(best_score, new_score)
    old_weight = jnp.exp(best_score - top_score)
    new_weight = jnp.exp(new_score - top_score)
    numerator = weighted * old_weight[..., None] + new_weight[..., None] * fresh_kv[:, :, 1].astype(
        jnp.float32
    )
    denominator = totals * old_weight + new_weight
    attention = (
        (numerator / denominator[..., None])
        .reshape(row_count, heads_here * HS)
        .astype(jnp.bfloat16)
    )
    base_output = lax.psum_scatter(
        lax.dot_general(
            out_weight, attention, (((0,), (1,)), ((), ())), preferred_element_type=jnp.float32
        ),
        "tp",
        scatter_dimension=0,
        tiled=True,
    ).T
    adapters_all = shrink_weight.shape[0]
    shrink_all = jnp.einsum(
        "rk,akq->raq", attention, shrink_weight, preferred_element_type=jnp.float32
    )
    chosen = adapter_id[:, None] == jnp.arange(adapters_all, dtype=jnp.int32)[None, :]
    partial_value = jnp.sum(jnp.where(chosen[:, :, None], shrink_all, 0.0), axis=1)
    shrink = lax.psum(partial_value, "tp").astype(jnp.bfloat16)
    spread = jnp.where(chosen[:, :, None], shrink[:, None, :], jnp.zeros((), jnp.bfloat16)).reshape(
        row_count, -1
    )
    expand_matrix = jnp.dot(
        spread, expand_weight.reshape(spread.shape[1], -1), preferred_element_type=jnp.float32
    )
    return (base_output + adapter_factor * expand_matrix).astype(jnp.bfloat16)


def remote(src, dst, send_sem, recv_sem, axis, target):
    return pltpu.make_async_remote_copy(
        src_ref=src,
        dst_ref=dst,
        send_sem=send_sem,
        recv_sem=recv_sem,
        device_id={axis: target},
        device_id_type=pl.DeviceIdType.MESH,
    )


def flipped(index, distance):
    bit, other = 1, index
    while bit <= distance:
        if distance & bit:
            other = other + bit - 2 * bit * lax.rem(index // bit, 2)
        bit *= 2
    return other


def as_column(row):
    size = row.shape[1]
    same = lax.broadcasted_iota(jnp.int32, (size, size), 0) == lax.broadcasted_iota(
        jnp.int32, (size, size), 1
    )
    return jnp.sum(jnp.where(same, row.astype(jnp.float32), 0.0), axis=1, keepdims=True)


def layer_kernel(
    n_tp,
    n_rep,
    rank,
    q_ref,
    new_ref,
    kv_hbm,
    owner_ref,
    fill_ref,
    mig_source_ref,
    mig_slot_ref,
    adapter_ref,
    out_w_hbm,
    shrink_w_hbm,
    expand_w_hbm,
    result_ref,
    kv,
    out_w,
    shrink_w,
    expand_w,
    q_all,
    slot_out,
    slot_in,
    slot_smem,
    mig_out,
    mig_in,
    acc_out,
    acc_in,
    stat_out,
    stat_in,
    shrink_out,
    shrink_in,
    base_out,
    base_in,
    sums,
    kv_sem,
    weight_sem,
    smem_sem,
    q_send,
    q_recv,
    slot_send,
    slot_recv,
    mig_send,
    mig_recv,
    acc_send,
    acc_recv,
    stat_send,
    stat_recv,
    shrink_send,
    shrink_recv,
    base_send,
    base_recv,
):
    f32, bf16 = jnp.float32, jnp.bfloat16
    tp = lax.axis_index("tp")
    rep = lax.axis_index("rep")
    rows = result_ref.shape[0]
    here = result_ref.shape[1]
    half = here // 2
    slots = kv.shape[0]
    migs = mig_out.shape[1]
    heads_here = here // HS
    own_rows = heads_here * rows
    group_size = H // KVH
    groups_here = heads_here // group_size
    group_rows = rows * group_size
    score_scale = 1.0 / math.sqrt(HS)
    middle = n_tp // 2
    tp_peers = [flipped(tp, d) for d in list(range(middle, n_tp)) + list(range(1, middle))]
    rep_peers = [lax.rem(rep + d, n_rep) for d in range(1, n_rep)]
    kv_copy = pltpu.make_async_copy(kv_hbm.at[0], kv, kv_sem)
    kv_copy.start()
    barrier = pltpu.get_barrier_semaphore()
    for peer in tp_peers:
        pl.semaphore_signal(
            barrier, inc=1, device_id={"tp": peer}, device_id_type=pl.DeviceIdType.MESH
        )
    for peer in rep_peers:
        pl.semaphore_signal(
            barrier, inc=1, device_id={"rep": peer}, device_id_type=pl.DeviceIdType.MESH
        )

    def block(k):
        return pl.ds(pl.multiple_of(k * here, here), here)

    def q_rows(k):
        return pl.ds(pl.multiple_of(k * own_rows, 16), own_rows)

    weight_copies = [pltpu.make_async_copy(shrink_w_hbm, shrink_w, weight_sem.at[0])]
    order = tp_peers + [tp]
    for i, peer in enumerate(order):
        weight_copies.append(
            pltpu.make_async_copy(
                out_w_hbm.at[:, block(peer)], out_w.at[:, block(peer)], weight_sem.at[1 + i]
            )
        )
    weight_copies.append(pltpu.make_async_copy(expand_w_hbm, expand_w, weight_sem.at[1 + n_tp]))
    for copy in weight_copies:
        copy.start()

    slot_lane = lax.broadcasted_iota(jnp.int32, slot_out.shape, 2)
    wanted = jnp.zeros(slot_out.shape, jnp.int32)
    for k in range(migs):
        wanted = jnp.where(slot_lane == k, mig_slot_ref[0, k], wanted)
    slot_out[...] = wanted
    slot_in[pl.ds(rep, 1)] = wanted
    own_query = q_ref[...].astype(f32)
    own_query = jnp.concatenate(
        [own_query[:, h * HS : (h + 1) * HS] for h in range(heads_here)], axis=0
    )
    q_all[q_rows(tp), :] = own_query.astype(bf16)
    mig_in[pl.ds(rep, 1)] = jnp.zeros((1,) + mig_in.shape[1:], bf16)
    pl.semaphore_wait(barrier, n_tp - 1 + n_rep - 1)

    slot_copies = [
        remote(
            slot_out, slot_in.at[pl.ds(rep, 1)], slot_send.at[d], slot_recv.at[d], "rep", peer
        )
        for d, peer in enumerate(rep_peers)
    ]
    for copy in slot_copies:
        copy.start()
    q_copies = [
        remote(q_all.at[q_rows(tp), :], q_all.at[q_rows(tp), :], q_send.at[d], q_recv.at[d], "tp", peer)
        for d, peer in enumerate(tp_peers)
    ]
    for copy in q_copies:
        copy.start()

    kv_copy.wait()
    for copy in slot_copies:
        copy.wait()
    to_smem = pltpu.make_async_copy(slot_in, slot_smem, smem_sem)
    to_smem.start()
    to_smem.wait()
    mig_copies = []
    for d, peer in enumerate(rep_peers):
        for k in range(migs):
            mig_out[d, k] = kv[slot_smem[peer, 0, k]]
        copy = remote(
            mig_out.at[d], mig_in.at[rep], mig_send.at[d], mig_recv.at[d], "rep", peer
        )
        copy.start()
        mig_copies.append(copy)

    fresh = new_ref[...].astype(f32)
    fresh_key = jnp.concatenate(
        [
            fresh[:, g * 2 * HS : (g * 2 + 1) * HS]
            for g in range(groups_here)
            for _ in range(group_size)
        ],
        axis=0,
    )
    fresh_value = jnp.concatenate(
        [
            fresh[:, (g * 2 + 1) * HS : (g * 2 + 2) * HS]
            for g in range(groups_here)
            for _ in range(group_size)
        ],
        axis=0,
    )
    new_score = jnp.sum(own_query * fresh_key, axis=1, keepdims=True) * score_scale
    row_index = lax.rem(lax.broadcasted_iota(jnp.int32, (group_rows, slots * BLK), 0), rows)
    slot_of = lax.broadcasted_iota(jnp.int32, (slots, slots * BLK), 1) // BLK
    spot = lax.rem(lax.broadcasted_iota(jnp.int32, (1, slots * BLK), 1), BLK).astype(f32)
    inside = slot_of == lax.broadcasted_iota(jnp.int32, (slots, slots * BLK), 0)
    owner, fill = [
        jnp.sum(jnp.where(inside, as_column(ref[...]), 0.0), axis=0, keepdims=True)
        for ref in (owner_ref, fill_ref)
    ]
    member = row_index.astype(f32) == jnp.where(spot < fill, owner, -1.0)
    adapter = as_column(adapter_ref[...])

    for copy in mig_copies:
        copy.wait()
    for k in range(migs):
        kv[slots - migs + k] = mig_in[mig_source_ref[0, k], k]

    acc_copies = []
    lane = lax.broadcasted_iota(jnp.int32, (group_rows, HS), 1)
    for d, peer in enumerate(order):
        if d < n_tp - 1:
            q_copies[d].wait_recv()
        stats = []
        for j in range(groups_here):
            group = peer * groups_here + j
            query = q_all[pl.ds(pl.multiple_of(group * group_rows, 16), group_rows), :]
            key_at = pl.ds(pl.multiple_of(group * 2 * HS, HS), HS)
            value_at = pl.ds(pl.multiple_of(group * 2 * HS + HS, HS), HS)
            key = kv[:, :, key_at].reshape(slots * BLK, HS)
            value = kv[:, :, value_at].reshape(slots * BLK, HS)
            score = (
                lax.dot_general(
                    query, key, (((1,), (1,)), ((), ())), preferred_element_type=f32
                )
                * score_scale
            )
            score = jnp.where(member, score, neg_big)
            top = jnp.max(score, axis=1, keepdims=True)
            weight = jnp.where(member, jnp.exp(score - top), 0.0)
            total = jnp.sum(weight, axis=1, keepdims=True)
            acc_out[d, j * group_rows : (j + 1) * group_rows, :] = jnp.dot(
                weight.astype(bf16), value, preferred_element_type=f32
            ).astype(bf16)
            stats.append(jnp.where(lane == 0, top, total))
            if d < n_tp - 1:
                part = pl.ds(j * group_rows, group_rows)
                copy = remote(
                    acc_out.at[d, part],
                    acc_in.at[d, part],
                    acc_send.at[d, j],
                    acc_recv.at[d, j],
                    "tp",
                    peer,
                )
                copy.start()
                acc_copies.append(copy)
        stat_out[d] = jnp.concatenate(stats, axis=0).T[:8]
        if d < n_tp - 1:
            copy = remote(
                stat_out.at[d], stat_in.at[d], stat_send.at[d], stat_recv.at[d], "tp", peer
            )
            copy.start()
            acc_copies.append(copy)
    for copy in q_copies:
        copy.wait_send()
    for copy in acc_copies:
        copy.wait()

    stat_rows = jnp.concatenate(
        [stat_in[d] for d in range(n_tp - 1)] + [stat_out[n_tp - 1]]
        + [jnp.zeros((HS - 8 * n_tp, own_rows), f32)],
        axis=0,
    )
    stat_columns = stat_rows.T
    tops = [stat_columns[:, 8 * d : 8 * d + 1] for d in range(n_tp)]
    totals = [stat_columns[:, 8 * d + 1 : 8 * d + 2] for d in range(n_tp)]
    best = functools.reduce(jnp.maximum, tops, new_score)
    fresh_ratio = jnp.exp(new_score - best)
    numerator = fresh_ratio * fresh_value
    denominator = fresh_ratio
    for d in range(n_tp):
        ratio = jnp.exp(tops[d] - best)
        part = acc_in[d] if d < n_tp - 1 else acc_out[d]
        numerator = numerator + ratio * part.astype(f32)
        denominator = denominator + ratio * totals[d]
    normal = numerator / denominator
    attention = jnp.concatenate(
        [normal[h * rows : (h + 1) * rows] for h in range(heads_here)], axis=1
    ).astype(bf16)

    def send_shrink():
        weight_copies[0].wait()
        chunk = 2 * HS
        folded = jnp.zeros((rank, rows), f32)
        for i in range(shrink_w.shape[0] // chunk):
            part = lax.dot_general(
                shrink_w[i * chunk : (i + 1) * chunk, :],
                attention,
                (((1,), (1,)), ((), ())),
                preferred_element_type=f32,
            )
            for j in range(chunk // rank):
                folded = folded + jnp.where(
                    adapter_ref[...] == i * (chunk // rank) + j,
                    part[j * rank : (j + 1) * rank],
                    0.0,
                )
        shrink_out[...] = folded
        copies = [
            remote(
                shrink_out, shrink_in.at[d], shrink_send.at[d], shrink_recv.at[d], "tp", peer
            )
            for d, peer in enumerate(tp_peers)
        ]
        for copy in copies:
            copy.start()
        return copies

    step = 256
    base_copies = []
    shrink_copies = []
    for d, peer in enumerate(order):
        if d == min(1, n_tp - 1):
            shrink_copies = send_shrink()
        weight_copies[1 + d].wait()

        def tile(i, carry, d=d, peer=peer):
            left = pl.multiple_of(peer * here + i * step, step)
            right = pl.multiple_of(peer * here + half + i * step, step)
            both = jnp.concatenate(
                [
                    jnp.dot(attention, out_w[:, pl.ds(at, step)], preferred_element_type=f32)
                    for at in (left, right)
                ],
                axis=0,
            )
            if d < n_tp - 1:
                base_out[d, :, pl.ds(pl.multiple_of(i * step, step), step)] = both.astype(bf16)
            else:
                sums[:, pl.ds(pl.multiple_of(i * step, step), step)] = both[:rows]
                sums[:, pl.ds(pl.multiple_of(half + i * step, step), step)] = both[rows:]
            return carry

        lax.fori_loop(0, half // step, tile, 0)
        if d < n_tp - 1:
            copy = remote(
                base_out.at[d], base_in.at[d], base_send.at[d], base_recv.at[d], "tp", peer
            )
            copy.start()
            base_copies.append(copy)

    for copy in shrink_copies:
        copy.wait()
    shrink = shrink_out[...]
    for d in range(n_tp - 1):
        shrink = shrink + shrink_in[d]
    per_lane = HS // rank
    shrink = jnp.concatenate([shrink] * per_lane, axis=0).T
    chunk_lane = lax.broadcasted_iota(jnp.int32, (rows, HS), 1)
    spread = jnp.concatenate(
        [
            jnp.where(adapter == (c * per_lane + chunk_lane // rank).astype(f32), shrink, 0.0)
            for c in range(shrink_w.shape[0] // HS)
        ],
        axis=1,
    ).astype(bf16)
    weight_copies[1 + n_tp].wait()

    def expand_tile(i, carry):
        at = pl.ds(pl.multiple_of(i * step, step), step)
        sums[:, at] = sums[:, at] + adapter_factor * jnp.dot(
            spread, expand_w[:, at], preferred_element_type=f32
        )
        return carry

    lax.fori_loop(0, here // step, expand_tile, 0)
    for copy in base_copies:
        copy.wait()
    left, right = sums[:, :half], sums[:, half:]
    for d in range(n_tp - 1):
        arrived = base_in[d].astype(f32)
        left = left + arrived[:rows]
        right = right + arrived[rows:]
    result_ref[:, :half] = left.astype(bf16)
    result_ref[:, half:] = right.astype(bf16)


def fused_body(
    queries,
    new_kv,
    kv_cache,
    slot_owner,
    slot_fill,
    mig_source,
    mig_slot,
    adapter_id,
    out_weight,
    shrink_weight,
    expand_weight,
):
    f32, bf16, i32 = jnp.float32, jnp.bfloat16, jnp.int32
    n_tp, n_rep = lax.axis_size("tp"), lax.axis_size("rep")
    rows, here = queries.shape
    heads_here = here // HS
    slots = kv_cache.shape[1]
    migs = mig_source.shape[1]
    width = kv_cache.shape[3]
    adapters, _, rank = shrink_weight.shape
    own_rows = rows * heads_here
    vmem = pl.BlockSpec(memory_space=pltpu.VMEM)
    smem = pl.BlockSpec(memory_space=pltpu.SMEM)
    hbm = pl.BlockSpec(memory_space=pl.ANY)
    dma = pltpu.SemaphoreType.DMA
    peers, others = n_tp - 1, n_rep - 1
    return pl.pallas_call(
        functools.partial(layer_kernel, n_tp, n_rep, rank),
        out_shape=jax.ShapeDtypeStruct((rows, here), bf16),
        in_specs=[vmem, vmem, hbm, vmem, vmem, smem, smem, vmem, hbm, hbm, hbm],
        out_specs=vmem,
        scratch_shapes=[
            pltpu.VMEM((slots, BLK, width), bf16),
            pltpu.VMEM(out_weight.shape, bf16),
            pltpu.VMEM((adapters * rank, here), bf16),
            pltpu.VMEM((adapters * rank, here), bf16),
            pltpu.VMEM((n_tp * own_rows, HS), bf16),
            pltpu.VMEM((1, 8, HS), i32),
            pltpu.VMEM((n_rep, 8, HS), i32),
            pltpu.SMEM((n_rep, 8, HS), i32),
            pltpu.VMEM((others, migs, BLK, width), bf16),
            pltpu.VMEM((n_rep, migs, BLK, width), bf16),
            pltpu.VMEM((n_tp, own_rows, HS), bf16),
            pltpu.VMEM((peers, own_rows, HS), bf16),
            pltpu.VMEM((n_tp, 8, own_rows), f32),
            pltpu.VMEM((peers, 8, own_rows), f32),
            pltpu.VMEM((rank, rows), f32),
            pltpu.VMEM((peers, rank, rows), f32),
            pltpu.VMEM((peers, 2 * rows, here // 2), bf16),
            pltpu.VMEM((peers, 2 * rows, here // 2), bf16),
            pltpu.VMEM((rows, here), f32),
            dma,
            dma((2 + n_tp,)),
            dma,
            dma((peers,)),
            dma((peers,)),
            dma((others,)),
            dma((others,)),
            dma((others,)),
            dma((others,)),
            dma((peers, heads_here * KVH // H)),
            dma((peers, heads_here * KVH // H)),
            dma((peers,)),
            dma((peers,)),
            dma((peers,)),
            dma((peers,)),
            dma((peers,)),
            dma((peers,)),
        ],
        compiler_params=pltpu.CompilerParams(
            collective_id=0, has_side_effects=True, vmem_limit_bytes=60 * 1024 * 1024
        ),
    )(
        queries,
        new_kv,
        kv_cache,
        slot_owner,
        slot_fill,
        mig_source,
        mig_slot,
        adapter_id[None, :],
        out_weight,
        shrink_weight.transpose(0, 2, 1).reshape(adapters * rank, here),
        expand_weight.reshape(adapters * rank, here),
    )


def solution(mesh):
    heads_here = H // mesh.shape["tp"]
    fits = heads_here % (H // KVH) == 0
    return jax.shard_map(
        fused_body if fits else body,
        mesh=mesh,
        in_specs=(
            P(("parts", "rep"), "tp"),
            P(("parts", "rep"), "tp"),
            P(("parts", "rep"), "tp", None, None),
            P(("parts", "rep"), "tp"),
            P(("parts", "rep"), "tp"),
            P(("parts", "rep"), "tp"),
            P(("parts", "rep"), "tp"),
            P(("parts", "rep")),
            P("tp", None),
            P(None, "tp", None),
            P(None, None, "tp"),
        ),
        out_specs=P(("parts", "rep"), "tp"),
        check_vma=False,
    )
```

```python
import functools
import math

import jax
import jax.numpy as jnp
from jax import lax
from jax.experimental import pallas as pl
from jax.experimental.pallas import tpu as pltpu
from jax.sharding import PartitionSpec as P

H = 64
KVH = 8
HS = 128
BLK = 16
MIGS = 2


neg_big = -1e30
adapter_factor = 2.0


def joined(shard, axis, combine):
    everything = jax.tree.map(lambda part: lax.all_gather(part, axis), shard)
    leading = jax.tree.map(lambda part: part[0], everything)

    def turn(k, so_far):
        return combine(so_far, jax.tree.map(lambda part: part[k], everything))

    return lax.fori_loop(1, lax.axis_size(axis), turn, leading)


def local_partials(kv_pool, slot_rows, slot_len, whole_queries):
    slot_count = kv_pool.shape[0]
    row_count = whole_queries.shape[0]
    group_size = H // KVH
    score_scale = 1.0 / math.sqrt(HS)
    query_rows = whole_queries.reshape(row_count, KVH, group_size, HS)
    blocks = kv_pool.reshape(slot_count, BLK, KVH, 2, HS)
    key_portion = blocks[:, :, :, 0]
    value_part = blocks[:, :, :, 1]
    is_owned = slot_rows >= 0
    slot_query = query_rows[jnp.maximum(slot_rows, 0)]
    scores = (
        jnp.einsum("sgjd,stgd->sgjt", slot_query, key_portion, preferred_element_type=jnp.float32)
        * score_scale
    )
    is_valid = (jnp.arange(BLK)[None, :] < slot_len[:, None]) & is_owned[:, None]
    scores = jnp.where(is_valid[:, None, None, :], scores, neg_big)
    slot_max = jnp.max(scores, axis=3)
    weights = jnp.where(is_valid[:, None, None, :], jnp.exp(scores - slot_max[..., None]), 0.0)
    slot_sum = jnp.sum(weights, axis=3)
    slot_acc = jnp.einsum(
        "sgjt,stgd->sgjd",
        weights.astype(jnp.bfloat16),
        value_part,
        preferred_element_type=jnp.float32,
    )
    member = slot_rows[None, :] == jnp.arange(row_count)[:, None]
    local_max = jnp.max(jnp.where(member[:, :, None, None], slot_max[None], neg_big), axis=1)
    rescale_factor = jnp.where(
        is_owned[:, None, None], jnp.exp(slot_max - local_max[jnp.maximum(slot_rows, 0)]), 0.0
    )
    onehot = member.astype(jnp.float32)
    totals = jnp.einsum(
        "rs,sgj->rgj", onehot, rescale_factor * slot_sum, precision=lax.Precision.HIGHEST
    )
    weighted = jnp.einsum(
        "rs,sgjd->rgjd",
        onehot,
        rescale_factor[..., None] * slot_acc,
        precision=lax.Precision.HIGHEST,
    )
    return (
        local_max.reshape(row_count, H),
        totals.reshape(row_count, H),
        weighted.reshape(row_count, H, HS),
    )


def combine(earlier, later):
    best_score = jnp.maximum(earlier[0], later[0])
    first_ratio = jnp.exp(earlier[0] - best_score)
    second_ratio = jnp.exp(later[0] - best_score)
    totals = earlier[1] * first_ratio + later[1] * second_ratio
    weighted = earlier[2] * first_ratio[..., None] + later[2] * second_ratio[..., None]
    return (best_score, totals, weighted)


def body(
    queries,
    new_kv,
    kv_cache,
    slot_owner,
    slot_fill,
    mig_source,
    mig_slot,
    adapter_id,
    out_weight,
    shrink_weight,
    expand_weight,
):
    row_count = queries.shape[0]
    heads_here = queries.shape[1] // HS
    group_size = H // KVH
    score_scale = 1.0 / math.sqrt(HS)
    whole_queries, whole_new = (
        lax.all_gather(queries, "tp", axis=1, tiled=True),
        lax.all_gather(new_kv, "tp", axis=1, tiled=True),
    )
    local_pool = kv_cache[0]
    slot_count = local_pool.shape[0]
    wanted_source, wanted_slot = (
        lax.all_gather(mig_source, "rep", axis=0, tiled=True),
        lax.all_gather(mig_slot, "rep", axis=0, tiled=True),
    )
    current_replica = lax.axis_index("rep")
    is_mine = wanted_source == current_replica
    packed = jnp.where(
        is_mine[:, :, None, None], local_pool[wanted_slot], jnp.zeros((), local_pool.dtype)
    )
    arrived = lax.all_to_all(packed, "rep", split_axis=0, concat_axis=0, tiled=True)
    copied = arrived[mig_source[0], jnp.arange(mig_source.shape[1])]
    kv_pool = local_pool.at[slot_count - MIGS :].set(copied)
    local_max, totals, weighted = local_partials(
        kv_pool, slot_owner[0], slot_fill[0], whole_queries
    )
    first_head = lax.axis_index("tp") * heads_here
    best_all, total_all, weight_all = joined((local_max, totals, weighted), "tp", combine)
    best_score = lax.dynamic_slice_in_dim(best_all, first_head, heads_here, 1)
    totals = lax.dynamic_slice_in_dim(total_all, first_head, heads_here, 1)
    weighted = lax.dynamic_slice_in_dim(weight_all, first_head, heads_here, 1)
    local_query = queries.reshape(row_count, heads_here, HS)
    groups = (first_head + jnp.arange(heads_here)) // group_size
    fresh_kv = jnp.take(whole_new.reshape(row_count, KVH, 2, HS), groups, axis=1)
    new_score = (
        jnp.einsum(
            "rhd,rhd->rh", local_query, fresh_kv[:, :, 0], preferred_element_type=jnp.float32
        )
        * score_scale
    )
    top_score = jnp.maximum(best_score, new_score)
    old_weight = jnp.exp(best_score - top_score)
    new_weight = jnp.exp(new_score - top_score)
    numerator = weighted * old_weight[..., None] + new_weight[..., None] * fresh_kv[:, :, 1].astype(
        jnp.float32
    )
    denominator = totals * old_weight + new_weight
    attention = (
        (numerator / denominator[..., None])
        .reshape(row_count, heads_here * HS)
        .astype(jnp.bfloat16)
    )
    base_output = lax.psum_scatter(
        lax.dot_general(
            out_weight, attention, (((0,), (1,)), ((), ())), preferred_element_type=jnp.float32
        ),
        "tp",
        scatter_dimension=0,
        tiled=True,
    ).T
    adapters_all = shrink_weight.shape[0]
    shrink_all = jnp.einsum(
        "rk,akq->raq", attention, shrink_weight, preferred_element_type=jnp.float32
    )
    chosen = adapter_id[:, None] == jnp.arange(adapters_all, dtype=jnp.int32)[None, :]
    partial_value = jnp.sum(jnp.where(chosen[:, :, None], shrink_all, 0.0), axis=1)
    shrink = lax.psum(partial_value, "tp").astype(jnp.bfloat16)
    spread = jnp.where(chosen[:, :, None], shrink[:, None, :], jnp.zeros((), jnp.bfloat16)).reshape(
        row_count, -1
    )
    expand_matrix = jnp.dot(
        spread, expand_weight.reshape(spread.shape[1], -1), preferred_element_type=jnp.float32
    )
    return (base_output + adapter_factor * expand_matrix).astype(jnp.bfloat16)


def remote(src, dst, send_sem, recv_sem, axis, target):
    return pltpu.make_async_remote_copy(
        src_ref=src,
        dst_ref=dst,
        send_sem=send_sem,
        recv_sem=recv_sem,
        device_id={axis: target},
        device_id_type=pl.DeviceIdType.MESH,
    )


def flipped(index, distance):
    bit, other = 1, index
    while bit <= distance:
        if distance & bit:
            other = other + bit - 2 * bit * lax.rem(index // bit, 2)
        bit *= 2
    return other


def as_column(row):
    size = row.shape[1]
    same = lax.broadcasted_iota(jnp.int32, (size, size), 0) == lax.broadcasted_iota(
        jnp.int32, (size, size), 1
    )
    return jnp.sum(jnp.where(same, row.astype(jnp.float32), 0.0), axis=1, keepdims=True)


def layer_kernel(
    n_tp,
    n_rep,
    rank,
    q_ref,
    new_ref,
    kv_hbm,
    owner_ref,
    fill_ref,
    mig_source_ref,
    mig_slot_ref,
    adapter_ref,
    out_w_hbm,
    shrink_w_hbm,
    expand_w_hbm,
    result_ref,
    kv,
    out_w,
    shrink_w,
    expand_w,
    q_all,
    slot_out,
    slot_in,
    slot_smem,
    mig_out,
    mig_in,
    acc_out,
    acc_in,
    stat_out,
    stat_in,
    shrink_out,
    shrink_in,
    base_out,
    base_in,
    sums,
    kv_sem,
    weight_sem,
    smem_sem,
    q_send,
    q_recv,
    slot_send,
    slot_recv,
    mig_send,
    mig_recv,
    acc_send,
    acc_recv,
    stat_send,
    stat_recv,
    shrink_send,
    shrink_recv,
    base_send,
    base_recv,
):
    f32, bf16 = jnp.float32, jnp.bfloat16
    tp = lax.axis_index("tp")
    rep = lax.axis_index("rep")
    rows = result_ref.shape[0]
    here = result_ref.shape[1]
    half = here // 2
    slots = kv.shape[0]
    migs = mig_out.shape[1]
    heads_here = here // HS
    own_rows = heads_here * rows
    group_size = H // KVH
    groups_here = heads_here // group_size
    group_rows = rows * group_size
    score_scale = 1.0 / math.sqrt(HS)
    middle = n_tp // 2
    tp_peers = [flipped(tp, d) for d in list(range(middle, n_tp)) + list(range(1, middle))]
    if n_rep & (n_rep - 1):
        rep_peers = [lax.rem(rep + d, n_rep) for d in range(1, n_rep)]
    else:
        far = n_rep // 2
        rep_peers = [flipped(rep, d) for d in list(range(far, n_rep)) + list(range(1, far))]
    kv_copy = pltpu.make_async_copy(kv_hbm.at[0], kv, kv_sem)
    kv_copy.start()
    barrier = pltpu.get_barrier_semaphore()
    for peer in tp_peers:
        pl.semaphore_signal(
            barrier, inc=1, device_id={"tp": peer}, device_id_type=pl.DeviceIdType.MESH
        )
    for peer in rep_peers:
        pl.semaphore_signal(
            barrier, inc=1, device_id={"rep": peer}, device_id_type=pl.DeviceIdType.MESH
        )

    def block(k):
        return pl.ds(pl.multiple_of(k * here, here), here)

    def q_rows(k):
        return pl.ds(pl.multiple_of(k * own_rows, 16), own_rows)

    weight_copies = [pltpu.make_async_copy(shrink_w_hbm, shrink_w, weight_sem.at[0])]
    order = tp_peers + [tp]
    for i, peer in enumerate(order):
        weight_copies.append(
            pltpu.make_async_copy(
                out_w_hbm.at[:, block(peer)], out_w.at[:, block(peer)], weight_sem.at[1 + i]
            )
        )
    weight_copies.append(pltpu.make_async_copy(expand_w_hbm, expand_w, weight_sem.at[1 + n_tp]))
    for copy in weight_copies:
        copy.start()

    slot_lane = lax.broadcasted_iota(jnp.int32, slot_out.shape, 2)
    wanted = jnp.zeros(slot_out.shape, jnp.int32)
    for k in range(migs):
        wanted = jnp.where(slot_lane == k, mig_slot_ref[0, k], wanted)
    slot_out[...] = wanted
    slot_in[pl.ds(rep, 1)] = wanted
    own_query = q_ref[...].astype(f32)
    own_query = jnp.concatenate(
        [own_query[:, h * HS : (h + 1) * HS] for h in range(heads_here)], axis=0
    )
    q_all[q_rows(tp), :] = own_query.astype(bf16)
    mig_in[pl.ds(rep, 1)] = jnp.zeros((1,) + mig_in.shape[1:], bf16)
    pl.semaphore_wait(barrier, n_tp - 1 + n_rep - 1)

    slot_copies = [
        remote(
            slot_out, slot_in.at[pl.ds(rep, 1)], slot_send.at[d], slot_recv.at[d], "rep", peer
        )
        for d, peer in enumerate(rep_peers)
    ]
    for copy in slot_copies:
        copy.start()
    q_copies = [
        remote(q_all.at[q_rows(tp), :], q_all.at[q_rows(tp), :], q_send.at[d], q_recv.at[d], "tp", peer)
        for d, peer in enumerate(tp_peers)
    ]
    for copy in q_copies:
        copy.start()

    kv_copy.wait()
    for copy in slot_copies:
        copy.wait()
    to_smem = pltpu.make_async_copy(slot_in, slot_smem, smem_sem)
    to_smem.start()
    to_smem.wait()
    mig_copies = []
    for d, peer in enumerate(rep_peers):
        for k in range(migs):
            mig_out[d, k] = kv[slot_smem[peer, 0, k]]
        copy = remote(
            mig_out.at[d], mig_in.at[rep], mig_send.at[d], mig_recv.at[d], "rep", peer
        )
        copy.start()
        mig_copies.append(copy)

    fresh = new_ref[...].astype(f32)
    fresh_key = jnp.concatenate(
        [
            fresh[:, g * 2 * HS : (g * 2 + 1) * HS]
            for g in range(groups_here)
            for _ in range(group_size)
        ],
        axis=0,
    )
    fresh_value = jnp.concatenate(
        [
            fresh[:, (g * 2 + 1) * HS : (g * 2 + 2) * HS]
            for g in range(groups_here)
            for _ in range(group_size)
        ],
        axis=0,
    )
    new_score = jnp.sum(own_query * fresh_key, axis=1, keepdims=True) * score_scale
    row_index = lax.rem(lax.broadcasted_iota(jnp.int32, (group_rows, slots * BLK), 0), rows)
    slot_of = lax.broadcasted_iota(jnp.int32, (slots, slots * BLK), 1) // BLK
    spot = lax.rem(lax.broadcasted_iota(jnp.int32, (1, slots * BLK), 1), BLK).astype(f32)
    inside = slot_of == lax.broadcasted_iota(jnp.int32, (slots, slots * BLK), 0)
    owner, fill = [
        jnp.sum(jnp.where(inside, as_column(ref[...]), 0.0), axis=0, keepdims=True)
        for ref in (owner_ref, fill_ref)
    ]
    member = row_index.astype(f32) == jnp.where(spot < fill, owner, -1.0)
    adapter = as_column(adapter_ref[...])

    for copy in mig_copies:
        copy.wait()
    for k in range(migs):
        kv[slots - migs + k] = mig_in[mig_source_ref[0, k], k]

    acc_copies = []
    lane = lax.broadcasted_iota(jnp.int32, (group_rows, HS), 1)
    for d, peer in enumerate(order):
        if d < n_tp - 1:
            q_copies[d].wait_recv()
        stats = []
        for j in range(groups_here):
            group = peer * groups_here + j
            query = q_all[pl.ds(pl.multiple_of(group * group_rows, 16), group_rows), :]
            key_at = pl.ds(pl.multiple_of(group * 2 * HS, HS), HS)
            value_at = pl.ds(pl.multiple_of(group * 2 * HS + HS, HS), HS)
            key = kv[:, :, key_at].reshape(slots * BLK, HS)
            value = kv[:, :, value_at].reshape(slots * BLK, HS)
            score = (
                lax.dot_general(
                    query, key, (((1,), (1,)), ((), ())), preferred_element_type=f32
                )
                * score_scale
            )
            score = jnp.where(member, score, neg_big)
            top = jnp.max(score, axis=1, keepdims=True)
            weight = jnp.where(member, jnp.exp(score - top), 0.0)
            total = jnp.sum(weight, axis=1, keepdims=True)
            acc_out[d, j * group_rows : (j + 1) * group_rows, :] = jnp.dot(
                weight.astype(bf16), value, preferred_element_type=f32
            ).astype(bf16)
            stats.append(jnp.where(lane == 0, top, total))
            if d < n_tp - 1:
                part = pl.ds(j * group_rows, group_rows)
                copy = remote(
                    acc_out.at[d, part],
                    acc_in.at[d, part],
                    acc_send.at[d, j],
                    acc_recv.at[d, j],
                    "tp",
                    peer,
                )
                copy.start()
                acc_copies.append(copy)
        stat_out[d] = jnp.concatenate(stats, axis=0).T[:8]
        if d < n_tp - 1:
            copy = remote(
                stat_out.at[d], stat_in.at[d], stat_send.at[d], stat_recv.at[d], "tp", peer
            )
            copy.start()
            acc_copies.append(copy)
    for copy in q_copies:
        copy.wait_send()
    for copy in acc_copies:
        copy.wait()

    stat_rows = jnp.concatenate(
        [stat_in[d] for d in range(n_tp - 1)] + [stat_out[n_tp - 1]]
        + [jnp.zeros((HS - 8 * n_tp, own_rows), f32)],
        axis=0,
    )
    stat_columns = stat_rows.T
    tops = [stat_columns[:, 8 * d : 8 * d + 1] for d in range(n_tp)]
    totals = [stat_columns[:, 8 * d + 1 : 8 * d + 2] for d in range(n_tp)]
    best = functools.reduce(jnp.maximum, tops, new_score)
    fresh_ratio = jnp.exp(new_score - best)
    numerator = fresh_ratio * fresh_value
    denominator = fresh_ratio
    for d in range(n_tp):
        ratio = jnp.exp(tops[d] - best)
        part = acc_in[d] if d < n_tp - 1 else acc_out[d]
        numerator = numerator + ratio * part.astype(f32)
        denominator = denominator + ratio * totals[d]
    normal = numerator / denominator
    attention = jnp.concatenate(
        [normal[h * rows : (h + 1) * rows] for h in range(heads_here)], axis=1
    ).astype(bf16)

    def send_shrink():
        weight_copies[0].wait()
        chunk = 2 * HS
        folded = jnp.zeros((rank, rows), f32)
        for i in range(shrink_w.shape[0] // chunk):
            part = lax.dot_general(
                shrink_w[i * chunk : (i + 1) * chunk, :],
                attention,
                (((1,), (1,)), ((), ())),
                preferred_element_type=f32,
            )
            for j in range(chunk // rank):
                folded = folded + jnp.where(
                    adapter_ref[...] == i * (chunk // rank) + j,
                    part[j * rank : (j + 1) * rank],
                    0.0,
                )
        shrink_out[...] = folded
        copies = [
            remote(
                shrink_out, shrink_in.at[d], shrink_send.at[d], shrink_recv.at[d], "tp", peer
            )
            for d, peer in enumerate(tp_peers)
        ]
        for copy in copies:
            copy.start()
        return copies

    step = 256
    base_copies = []
    shrink_copies = []
    for d, peer in enumerate(order):
        if d == min(1, n_tp - 1):
            shrink_copies = send_shrink()
        weight_copies[1 + d].wait()

        def tile(i, carry, d=d, peer=peer):
            left = pl.multiple_of(peer * here + i * step, step)
            right = pl.multiple_of(peer * here + half + i * step, step)
            both = jnp.concatenate(
                [
                    jnp.dot(attention, out_w[:, pl.ds(at, step)], preferred_element_type=f32)
                    for at in (left, right)
                ],
                axis=0,
            )
            if d < n_tp - 1:
                base_out[d, :, pl.ds(pl.multiple_of(i * step, step), step)] = both.astype(bf16)
            else:
                sums[:, pl.ds(pl.multiple_of(i * step, step), step)] = both[:rows]
                sums[:, pl.ds(pl.multiple_of(half + i * step, step), step)] = both[rows:]
            return carry

        lax.fori_loop(0, half // step, tile, 0)
        if d < n_tp - 1:
            copy = remote(
                base_out.at[d], base_in.at[d], base_send.at[d], base_recv.at[d], "tp", peer
            )
            copy.start()
            base_copies.append(copy)

    for copy in shrink_copies:
        copy.wait()
    shrink = shrink_out[...]
    for d in range(n_tp - 1):
        shrink = shrink + shrink_in[d]
    per_lane = HS // rank
    shrink = jnp.concatenate([shrink] * per_lane, axis=0).T
    chunk_lane = lax.broadcasted_iota(jnp.int32, (rows, HS), 1)
    spread = jnp.concatenate(
        [
            jnp.where(adapter == (c * per_lane + chunk_lane // rank).astype(f32), shrink, 0.0)
            for c in range(shrink_w.shape[0] // HS)
        ],
        axis=1,
    ).astype(bf16)
    weight_copies[1 + n_tp].wait()

    def expand_tile(i, carry):
        at = pl.ds(pl.multiple_of(i * step, step), step)
        sums[:, at] = sums[:, at] + adapter_factor * jnp.dot(
            spread, expand_w[:, at], preferred_element_type=f32
        )
        return carry

    lax.fori_loop(0, here // step, expand_tile, 0, unroll=True)
    for copy in base_copies:
        copy.wait()
    left, right = sums[:, :half], sums[:, half:]
    for d in range(n_tp - 1):
        arrived = base_in[d].astype(f32)
        left = left + arrived[:rows]
        right = right + arrived[rows:]
    result_ref[:, :half] = left.astype(bf16)
    result_ref[:, half:] = right.astype(bf16)


def fused_body(
    queries,
    new_kv,
    kv_cache,
    slot_owner,
    slot_fill,
    mig_source,
    mig_slot,
    adapter_id,
    out_weight,
    shrink_weight,
    expand_weight,
):
    f32, bf16, i32 = jnp.float32, jnp.bfloat16, jnp.int32
    n_tp, n_rep = lax.axis_size("tp"), lax.axis_size("rep")
    rows, here = queries.shape
    heads_here = here // HS
    slots = kv_cache.shape[1]
    migs = mig_source.shape[1]
    width = kv_cache.shape[3]
    adapters, _, rank = shrink_weight.shape
    own_rows = rows * heads_here
    vmem = pl.BlockSpec(memory_space=pltpu.VMEM)
    smem = pl.BlockSpec(memory_space=pltpu.SMEM)
    hbm = pl.BlockSpec(memory_space=pl.ANY)
    dma = pltpu.SemaphoreType.DMA
    peers, others = n_tp - 1, n_rep - 1
    return pl.pallas_call(
        functools.partial(layer_kernel, n_tp, n_rep, rank),
        out_shape=jax.ShapeDtypeStruct((rows, here), bf16),
        in_specs=[vmem, vmem, hbm, vmem, vmem, smem, smem, vmem, hbm, hbm, hbm],
        out_specs=vmem,
        scratch_shapes=[
            pltpu.VMEM((slots, BLK, width), bf16),
            pltpu.VMEM(out_weight.shape, bf16),
            pltpu.VMEM((adapters * rank, here), bf16),
            pltpu.VMEM((adapters * rank, here), bf16),
            pltpu.VMEM((n_tp * own_rows, HS), bf16),
            pltpu.VMEM((1, 8, HS), i32),
            pltpu.VMEM((n_rep, 8, HS), i32),
            pltpu.SMEM((n_rep, 8, HS), i32),
            pltpu.VMEM((others, migs, BLK, width), bf16),
            pltpu.VMEM((n_rep, migs, BLK, width), bf16),
            pltpu.VMEM((n_tp, own_rows, HS), bf16),
            pltpu.VMEM((peers, own_rows, HS), bf16),
            pltpu.VMEM((n_tp, 8, own_rows), f32),
            pltpu.VMEM((peers, 8, own_rows), f32),
            pltpu.VMEM((rank, rows), f32),
            pltpu.VMEM((peers, rank, rows), f32),
            pltpu.VMEM((peers, 2 * rows, here // 2), bf16),
            pltpu.VMEM((peers, 2 * rows, here // 2), bf16),
            pltpu.VMEM((rows, here), f32),
            dma,
            dma((2 + n_tp,)),
            dma,
            dma((peers,)),
            dma((peers,)),
            dma((others,)),
            dma((others,)),
            dma((others,)),
            dma((others,)),
            dma((peers, heads_here * KVH // H)),
            dma((peers, heads_here * KVH // H)),
            dma((peers,)),
            dma((peers,)),
            dma((peers,)),
            dma((peers,)),
            dma((peers,)),
            dma((peers,)),
        ],
        compiler_params=pltpu.CompilerParams(
            collective_id=0, has_side_effects=True, vmem_limit_bytes=60 * 1024 * 1024
        ),
    )(
        queries,
        new_kv,
        kv_cache,
        slot_owner,
        slot_fill,
        mig_source,
        mig_slot,
        adapter_id[None, :],
        out_weight,
        shrink_weight.transpose(0, 2, 1).reshape(adapters * rank, here),
        expand_weight.reshape(adapters * rank, here),
    )


def solution(mesh):
    heads_here = H // mesh.shape["tp"]
    fits = heads_here % (H // KVH) == 0
    return jax.shard_map(
        fused_body if fits else body,
        mesh=mesh,
        in_specs=(
            P(("parts", "rep"), "tp"),
            P(("parts", "rep"), "tp"),
            P(("parts", "rep"), "tp", None, None),
            P(("parts", "rep"), "tp"),
            P(("parts", "rep"), "tp"),
            P(("parts", "rep"), "tp"),
            P(("parts", "rep"), "tp"),
            P(("parts", "rep")),
            P("tp", None),
            P(None, "tp", None),
            P(None, None, "tp"),
        ),
        out_specs=P(("parts", "rep"), "tp"),
        check_vma=False,
    )
```
